512 devices in a mesh: rep: 16 (over z_hi, y), fsdp: 32 (over z_lo, x, core).
Axes of the slice: x: 4, y: 4, z: 16 (z_hi: 4, z_lo: 4; z = z_hi * 4 + z_lo), core: 2. Of those that a mesh axis runs over, the one named last changes fastest.
Arguments:
- grad_parts: bfloat16 [16, 32, 128, 8192], P('rep', 'fsdp'), may hold values from -6 to 6
- momentum: float32 [16, 128, 8192], P('rep', None, 'fsdp'), may hold values from -6 to 6
Outputs:
- momentum_out: float32 [16, 128, 8192], P('rep', None, 'fsdp')
- update: float32 [128, 8192], P(None, 'fsdp')
The draws below stay inside these ranges and needn't reach their ends.
All inputs are finite; a program needn't handle non-finite values.
Results may differ from the reference program's by a relative error of at most 0.0003.
Values sent between devices are 32-bit elements; how exact they have to be, the bound alone decides.
A program may use at most 64 MiB of HBM per device.

```python
import jax
import jax.numpy as jnp
from jax import lax

GROUP = 64
BAND = 8
RB = 2
ROWS = 128
COLS = 8192
N_REP = 16
N_FSDP = 32


def strengthened(entries, rng, source, target, parts, factor):
    def block_of(axis_at):
        return (jnp.arange(entries.shape[axis_at]) // (entries.shape[axis_at] // parts)).reshape((-1,) + (1,) * (entries.ndim - 1 - axis_at))

    first = jax.random.permutation(rng, parts)[block_of(target)]
    far = (block_of(target) + parts // 2) % parts
    return jnp.where((block_of(source) == first) | (block_of(source) == far), factor * entries, entries)


def block_scale(key, extent, cuts, least, top_value):
    def one(position, parts):
        heights = jax.random.uniform(jax.random.fold_in(jax.random.fold_in(key, 6), position), (parts,), jnp.float32, least / len(cuts), top_value / len(cuts))
        return jnp.repeat(jnp.exp(heights), extent[position] // parts).reshape((-1,) + (1,) * (len(extent) - position - 1))

    loudness = one(*cuts[0])
    for cut in cuts[1:]:
        loudness = loudness * one(*cut)
    return loudness


def bell_draw(own_key, shape, deviation, bound, shards=(), held_as=jnp.bfloat16):
    array = deviation * jax.random.normal(own_key, shape, jnp.float32)
    if shards:
        array = array * block_scale(own_key, shape, shards, -0.22, 0.18)
    return jnp.clip(array, -bound, bound).astype(held_as)


def heavy_noise(stream_key, dims, scale, reach, shards, heavy, held_as=jnp.bfloat16):
    drawn = scale * jax.random.normal(stream_key, dims, jnp.float32)
    if shards:
        drawn = drawn * block_scale(stream_key, dims, shards, -0.22, 0.18)
    return jnp.clip(strengthened(drawn, jax.random.fold_in(stream_key, 3), *heavy), -reach, reach).astype(held_as)


def setup_inputs(seed: int = 0) -> dict:
    key_list = jax.random.split(jax.random.key(seed), 3)
    return {
        "grad_parts": heavy_noise(key_list[0], (N_REP, N_FSDP, ROWS, COLS), 0.2, 6.0, ((0, 16), (1, 32)), (1, 3, 32, 2.75)),
        "momentum": bell_draw(key_list[1], (N_REP, ROWS, COLS), 1.0, 6.0, ((0, 16), (2, 32)), jnp.float32),
    }


def make_basis():
    freq = jnp.arange(BAND, dtype=jnp.float32)[:, None]
    place = jnp.arange(GROUP, dtype=jnp.float32)[None, :]
    scale = jnp.where(freq == 0.0, jnp.sqrt(1.0 / GROUP), jnp.sqrt(2.0 / GROUP)).astype(jnp.float32)
    return (scale * jnp.cos(jnp.pi * (2.0 * place + 1.0) * freq / (2.0 * GROUP))).astype(jnp.float32)

def band_of(field, basis):
    ncol = field.shape[1] // GROUP
    blocks = field.reshape(RB, GROUP, ncol, GROUP)
    left = jnp.einsum('ka,iajb->ikjb', basis, blocks, precision=lax.Precision.HIGHEST)
    both = jnp.einsum('ikjb,lb->ikjl', left, basis, precision=lax.Precision.HIGHEST)
    return both.reshape(RB * BAND, ncol * BAND)

def back_of(coeffs, basis):
    ncol = coeffs.shape[1] // BAND
    blocks = coeffs.reshape(RB, BAND, ncol, BAND)
    left = jnp.einsum('ka,ikjl->iajl', basis, blocks, precision=lax.Precision.HIGHEST)
    both = jnp.einsum('iajl,lb->iajb', left, basis, precision=lax.Precision.HIGHEST)
    return both.reshape(RB * GROUP, ncol * GROUP)

def reference(grad_parts, momentum):
    basis = make_basis()

    def replica(index):
        grad = lax.optimization_barrier(jnp.sum(grad_parts[index].astype(jnp.float32), axis=0))
        moment = 0.999 * momentum[index] + grad
        band = band_of(moment, basis)
        return (moment - back_of(band, basis), band)
    momentum_out, bands = lax.map(replica, jnp.arange(N_REP, dtype=jnp.int32))
    shared = lax.optimization_barrier(jnp.sum(bands, axis=0)) / N_REP
    update = back_of(shared, basis)
    return (momentum_out, update)
```

```python
import jax
import jax.numpy as jnp
import numpy as np
from jax import lax
from jax.experimental import pallas as pl
from jax.experimental.pallas import tpu as pltpu
from jax.sharding import PartitionSpec as P

MESH = pl.DeviceIdType.MESH
F32, BF16 = jnp.float32, jnp.bfloat16
GROUP, BAND = 64, 8
ROWS, WIDTH = 128, 256
NX = NY = NL = NH = 4

PIECES = ((0, 32), (32, 32), (64, 32), (96, 32))
K = len(PIECES)
FAR, NEXT, PREV, OWN = 0, 1, 2, 3
STEP_OF_SLOT = (2, 1, 3, 0)


def tables():
    freq = np.arange(BAND)[:, None]
    place = np.arange(GROUP)[None, :]
    scale = np.where(freq == 0, np.sqrt(1.0 / GROUP), np.sqrt(2.0 / GROUP))
    basis = (scale * np.cos(np.pi * (2 * place + 1) * freq / (2 * GROUP))).astype(np.float32)
    rows = np.kron(np.eye(ROWS // GROUP, dtype=np.float32), basis)
    cols = np.kron(np.eye(WIDTH // GROUP, dtype=np.float32), basis).T
    spread = np.zeros((NX, WIDTH, 128), np.float32)
    for q in range(NX):
        spread[q, :, q * 32 : (q + 1) * 32] = cols
    return rows, spread


def split(value):
    high = value.astype(BF16)
    return high, (value - high.astype(F32)).astype(BF16)


def dot(a, b):
    return jnp.dot(a, b, preferred_element_type=F32)


def exact(a, b, dims):
    return lax.dot_general(a, b, (dims, ((), ())), precision=lax.Precision.HIGHEST, preferred_element_type=F32)


def kernel(
    grad_hbm, mom_hbm, rows_hbm, pair_hbm, spread_hbm, wide_hbm, mo_hbm, up_hbm,
    grad, mom, rows_t, pair_t, spread_t, wide_t, give, part, far_p, far_m, near_p, near_m, from_z,
    bands, bands_c, bands_z, bands_x, bands_y, bands_h, rest, mo, up,
    load_sem, out_sem, core_ss, core_rs, x_ss, x_rs, z_ss, z_rs, b_ss, b_rs, know,
):
    rep, f = lax.axis_index("rep"), lax.axis_index("fsdp")
    zh, y = rep // NY, rep % NY
    zl, x, c = f // (2 * NX), (f // 2) % NX, f % 2
    z = zh * NL + zl

    def device(dx=0, dy=0, dl=0, dz=0, dc=0):
        zz = (z + dz + NL * NH) % (NL * NH)
        low = (zz % NL + dl) % NL
        to_rep = (zz // NL) * NY + (y + dy + NY) % NY
        to_f = (low * NX + (x + dx + NX) % NX) * 2 + (c + dc) % 2
        return to_rep, to_f

    def signal(sem, **where):
        pl.semaphore_signal(sem, inc=1, device_id=device(**where), device_id_type=MESH)

    def send(src, dst, ss, rs, **where):
        copy = pltpu.make_async_remote_copy(
            src_ref=src, dst_ref=dst, send_sem=ss, recv_sem=rs, device_id=device(**where), device_id_type=MESH
        )
        copy.start()
        return copy

    barrier = pltpu.get_barrier_semaphore()
    near = (dict(dc=1), dict(dx=1), dict(dx=-1), dict(dy=1), dict(dy=-1), dict(dz=1), dict(dz=-1))
    for where in near:
        signal(barrier, **where)

    loads = [
        pltpu.make_async_copy(grad_hbm.at[0, 0, pl.ds(r0, n)], grad.at[pl.ds(r0, n)], load_sem.at[k])
        for k, (r0, n) in enumerate(PIECES)
    ]
    extra = [
        pltpu.make_async_copy(src, dst, load_sem.at[K + i])
        for i, (src, dst) in enumerate(
            ((rows_hbm, rows_t), (pair_hbm, pair_t), (spread_hbm, spread_t), (wide_hbm, wide_t), (mom_hbm.at[0], mom))
        )
    ]
    for copy in loads + extra:
        copy.start()

    def columns(slot, dl, core):
        owner = (((zl + dl) % NL) * NX + (x + STEP_OF_SLOT[slot]) % NX) * 2 + core
        return pl.ds(pl.multiple_of(owner * WIDTH, WIDTH), WIDTH)

    def convert(k):
        r0, n = PIECES[k]
        for slot in range(4):
            for dl in range(NL):
                give[slot, dl, pl.ds(r0, n)] = grad[pl.ds(r0, n), columns(slot, dl, 1 - c)].astype(F32)

    def add_own(k, slot):
        r0, n = PIECES[k]
        for dl in range(NL):
            part[slot, dl, pl.ds(r0, n)] += grad[pl.ds(r0, n), columns(slot, dl, c)].astype(F32)

    sent = []
    core_far, core_rest = {}, {}

    def give_piece(k):
        r0, n = PIECES[k]
        rows = pl.ds(r0, n)
        core_far[k] = send(
            give.at[pl.ds(FAR, 1), :, rows], part.at[pl.ds(FAR, 1), :, rows], core_ss.at[2 * k], core_rs.at[2 * k], dc=1
        )
        core_rest[k] = send(
            give.at[pl.ds(1, 3), :, rows], part.at[pl.ds(1, 3), :, rows], core_ss.at[2 * k + 1], core_rs.at[2 * k + 1], dc=1
        )
        sent.extend((core_far[k], core_rest[k]))

    loads[0].wait()
    convert(0)
    pl.semaphore_wait(barrier, len(near))
    give_piece(0)
    signal(know.at[0], dx=1)
    signal(know.at[1], dy=1)
    signal(know.at[2], dz=1)
    signal(know.at[3], dz=-1)
    for k in range(1, K):
        loads[k].wait()
        convert(k)
        give_piece(k)

    fars, nears, adds, zs = {}, {}, {}, {}

    def halves(k):
        r0, n = PIECES[k]
        return pl.ds(r0, n // 2), pl.ds(r0 + n // 2, n // 2), pl.ds(r0 // 2, n // 2)

    def open_piece(k):
        lower, upper, packed = halves(k)
        core_far[k].wait_recv()
        add_own(k, FAR)
        fars[k] = (
            send(part.at[FAR, :, lower], far_p.at[:, packed], x_ss.at[6 * k], x_rs.at[6 * k], dx=1),
            send(part.at[FAR, :, upper], far_m.at[:, packed], x_ss.at[6 * k + 1], x_rs.at[6 * k + 1], dx=-1),
        )
        core_rest[k].wait_recv()
        add_own(k, NEXT)
        add_own(k, PREV)
        nears[k] = (
            send(part.at[NEXT, :, upper], near_p.at[:, upper], x_ss.at[6 * k + 2], x_rs.at[6 * k + 2], dx=1),
            send(part.at[PREV, :, lower], near_m.at[:, lower], x_ss.at[6 * k + 3], x_rs.at[6 * k + 3], dx=-1),
        )
        add_own(k, OWN)
        sent.extend(fars[k] + nears[k])

    def pass_on(k):
        lower, upper, packed = halves(k)
        fars[k][0].wait_recv()
        part[NEXT, :, lower] += far_p[:, packed]
        first = send(part.at[NEXT, :, lower], near_p.at[:, lower], x_ss.at[6 * k + 4], x_rs.at[6 * k + 4], dx=1)
        fars[k][1].wait_recv()
        part[PREV, :, upper] += far_m[:, packed]
        second = send(part.at[PREV, :, upper], near_m.at[:, upper], x_ss.at[6 * k + 5], x_rs.at[6 * k + 5], dx=-1)
        adds[k] = (first, second)
        sent.extend(adds[k])

    def along_z(k):
        r0, n = PIECES[k]
        rows = pl.ds(r0, n)
        for copy in nears[k] + adds[k]:
            copy.wait_recv()
        zs[k] = []
        for dl in (3, 2, 1, 0):
            part[OWN, dl, rows] += near_p[dl, rows] + near_m[dl, rows]
            if dl:
                zs[k].append(
                    send(part.at[OWN, dl, rows], from_z.at[dl - 1, rows], z_ss.at[3 * k + dl - 1], z_rs.at[3 * k + dl - 1], dl=dl)
                )
        sent.extend(zs[k])

    outs = []

    def close(k):
        r0, n = PIECES[k]
        rows = pl.ds(r0, n)
        for copy in zs[k]:
            copy.wait_recv()
        mo[rows] = rest[rows] + ((part[OWN, 0, rows] + from_z[0, rows]) + (from_z[1, rows] + from_z[2, rows]))
        copy = pltpu.make_async_copy(mo.at[rows], mo_hbm.at[0, rows], out_sem.at[k])
        copy.start()
        outs.append(copy)

    def band_parts():
        for core in range(2):
            which = core
            owner_core = (c + core) % 2
            for dl in range(NL):
                total = jnp.zeros((2 * 16, 256), F32)
                for q in range(NX):
                    owner = (((zl + dl) % NL) * NX + q) * 2 + owner_core
                    block = grad[:, pl.ds(pl.multiple_of(owner * WIDTH, WIDTH), WIDTH)]
                    left = dot(pair_t[...], block)
                    high, low = split(left[:16] + left[16:])
                    total += dot(jnp.concatenate([high, low], axis=0), wide_t[q])
                bands[which, dl] = total[:16, :128] + total[:16, 128:] + total[16:, :128]

    def inverse(coeffs):
        return exact(rows_t[...], exact(coeffs, spread_t[x], ((1,), (1,))), ((0,), (0,)))

    def band_core():
        copy = send(bands.at[1], bands_c, b_ss.at[0], b_rs.at[0], dc=1)
        sent.append(copy)
        return copy

    def band_z(copy):
        copy.wait_recv()
        bands_c[...] += bands[0]
        copies = []
        for dl in (1, 2, 3):
            copies.append(send(bands_c.at[dl], bands_z.at[dl - 1], b_ss.at[dl], b_rs.at[dl], dl=dl))
        sent.extend(copies)
        return copies

    def band_x(copies):
        for copy in copies:
            copy.wait_recv()
        bands_x[0] = (bands_c[0] + bands_z[0]) + (bands_z[1] + bands_z[2])
        out = []
        for dx in (1, 2, 3):
            out.append(send(bands_x.at[0], bands_x.at[dx], b_ss.at[3 + dx], b_rs.at[3 + dx], dx=dx))
        sent.extend(out)
        return out

    def band_y(copies):
        for copy in copies:
            copy.wait_recv()
        total = (bands_x[0] + bands_x[1]) + (bands_x[2] + bands_x[3])
        own = exact(exact(rows_t[...], mom[...], ((1,), (0,))), spread_t[x], ((1,), (0,)))
        total = total + 0.999 * own
        bands_y[y] = total
        out = []
        for dy in (1, 2, 3):
            out.append(send(bands_y.at[y], bands_y.at[y], b_ss.at[6 + dy], b_rs.at[6 + dy], dy=dy))
        sent.extend(out)
        rest[...] = 0.999 * mom[...] - inverse(total)
        return out

    def band_h(copies):
        for copy in copies:
            copy.wait_recv()
        bands_h[zh] = (bands_y[0] + bands_y[1]) + (bands_y[2] + bands_y[3])
        out = []
        for dh in (1, 2, 3):
            out.append(send(bands_h.at[zh], bands_h.at[zh], b_ss.at[9 + dh], b_rs.at[9 + dh], dz=NL * dh))
        sent.extend(out)
        return out

    def band_end(copies):
        for copy in copies:
            copy.wait_recv()
        shared = ((bands_h[0] + bands_h[1]) + (bands_h[2] + bands_h[3])) * (1.0 / (NY * NH))
        up[...] = inverse(shared)
        copy = pltpu.make_async_copy(up, up_hbm, out_sem.at[K])
        copy.start()
        outs.append(copy)

    open_piece(0)
    for copy in extra:
        copy.wait()
    band_parts()
    b = band_core()
    pl.semaphore_wait(know.at[2], 1)
    pl.semaphore_wait(know.at[3], 1)
    signal(know.at[4], dz=1)
    signal(know.at[5], dz=-1)
    signal(know.at[6], dz=2)
    signal(know.at[7], dz=-2)
    open_piece(1)
    pass_on(0)
    pl.semaphore_wait(know.at[4], 1)
    pl.semaphore_wait(know.at[5], 1)
    b = band_z(b)
    open_piece(2)
    pass_on(1)
    pl.semaphore_wait(know.at[6], 1)
    pl.semaphore_wait(know.at[7], 1)
    signal(know.at[8], dz=4)
    along_z(0)
    pl.semaphore_wait(know.at[0], 1)
    b = band_x(b)
    open_piece(3)
    pass_on(2)
    along_z(1)
    pl.semaphore_wait(know.at[1], 1)
    b = band_y(b)
    pass_on(3)
    along_z(2)
    pl.semaphore_wait(know.at[8], 1)
    b = band_h(b)
    close(0)
    along_z(3)
    close(1)
    close(2)
    close(3)
    band_end(b)
    for copy in sent:
        copy.wait_send()
    for copy in outs:
        copy.wait()


def body(grad_parts, momentum):
    rows, spread = tables()
    rows_high = rows.astype(jnp.bfloat16)
    rows_low = (rows - rows_high.astype(np.float32)).astype(jnp.bfloat16)
    pair = np.concatenate([rows_high, rows_low], axis=0)
    spread_high = spread.astype(jnp.bfloat16)
    spread_low = (spread - spread_high.astype(np.float32)).astype(jnp.bfloat16)
    wide = np.concatenate([spread_high, spread_low], axis=2)
    any_space = pl.BlockSpec(memory_space=pl.ANY)
    vmem = pltpu.VMEM
    dma = pltpu.SemaphoreType.DMA
    out = pl.pallas_call(
        kernel,
        out_shape=(jax.ShapeDtypeStruct((1, ROWS, WIDTH), F32), jax.ShapeDtypeStruct((ROWS, WIDTH), F32)),
        in_specs=[any_space] * 6,
        out_specs=(any_space, any_space),
        scratch_shapes=[
            vmem((ROWS, 8192), BF16),
            vmem((ROWS, WIDTH), F32),
            vmem((16, ROWS), F32),
            vmem((32, ROWS), BF16),
            vmem((NX, WIDTH, 128), F32),
            vmem((NX, WIDTH, 256), BF16),
            vmem((4, NL, ROWS, WIDTH), F32),
            vmem((4, NL, ROWS, WIDTH), F32),
            vmem((NL, ROWS // 2, WIDTH), F32),
            vmem((NL, ROWS // 2, WIDTH), F32),
            vmem((NL, ROWS, WIDTH), F32),
            vmem((NL, ROWS, WIDTH), F32),
            vmem((3, ROWS, WIDTH), F32),
            vmem((2, NL, 16, 128), F32),
            vmem((NL, 16, 128), F32),
            vmem((3, 16, 128), F32),
            vmem((4, 16, 128), F32),
            vmem((4, 16, 128), F32),
            vmem((4, 16, 128), F32),
            vmem((ROWS, WIDTH), F32),
            vmem((ROWS, WIDTH), F32),
            vmem((ROWS, WIDTH), F32),
            dma((K + 5,)),
            dma((K + 1,)),
            dma((2 * K,)),
            dma((2 * K,)),
            dma((6 * K,)),
            dma((6 * K,)),
            dma((3 * K,)),
            dma((3 * K,)),
            dma((13,)),
            dma((13,)),
            pltpu.SemaphoreType.REGULAR((9,)),
        ],
        compiler_params=pltpu.CompilerParams(collective_id=0, has_side_effects=True, vmem_limit_bytes=60 * 2**20),
    )(
        grad_parts, momentum, jnp.asarray(rows), jnp.asarray(pair), jnp.asarray(spread), jnp.asarray(wide)
    )
    return out


def solution(mesh):
    in_specs = (P("rep", "fsdp", None, None), P("rep", None, "fsdp"))
    out_specs = (P("rep", None, "fsdp"), P(None, "fsdp"))
    return jax.shard_map(body, mesh=mesh, in_specs=in_specs, out_specs=out_specs, check_vma=False)
```

```python
import jax
import jax.numpy as jnp
import numpy as np
from jax import lax
from jax.experimental import pallas as pl
from jax.experimental.pallas import tpu as pltpu
from jax.sharding import PartitionSpec as P

MESH = pl.DeviceIdType.MESH
F32, BF16 = jnp.float32, jnp.bfloat16
GROUP, BAND = 64, 8
ROWS, WIDTH = 128, 256
NX = NY = NL = NH = 4

PIECES = ((0, 32), (32, 32), (64, 32), (96, 32))
K = len(PIECES)
FAR, NEXT, PREV, OWN = 0, 1, 2, 3
STEP_OF_SLOT = (2, 1, 3, 0)


def tables():
    freq = np.arange(BAND)[:, None]
    place = np.arange(GROUP)[None, :]
    scale = np.where(freq == 0, np.sqrt(1.0 / GROUP), np.sqrt(2.0 / GROUP))
    basis = (scale * np.cos(np.pi * (2 * place + 1) * freq / (2 * GROUP))).astype(np.float32)
    rows = np.kron(np.eye(ROWS // GROUP, dtype=np.float32), basis)
    cols = np.kron(np.eye(WIDTH // GROUP, dtype=np.float32), basis).T
    wide = np.zeros((2 * WIDTH, 128), np.float32)
    wide[:WIDTH, :32] = cols
    wide[WIDTH:, 32:64] = cols
    return basis, rows, wide


def split(value):
    high = value.astype(BF16)
    return high, (value - high.astype(F32)).astype(BF16)


def dot(a, b):
    return jnp.dot(a, b, preferred_element_type=F32)


def exact(a, b, dims):
    return lax.dot_general(a, b, (dims, ((), ())), precision=lax.Precision.HIGHEST, preferred_element_type=F32)


def kernel(
    grad_hbm, mom_hbm, basis_hbm, rows_hbm, wide_hbm, out, grad, mom, basis_t, rows_t, wide_t, give, part,
    far_p, far_m, near_p, near_m, from_z, left_t, bands, bands_c, bands_z, sums_z, bands_xy, sums_y, bands_h, rest,
    load_sem, core_ss, core_rs, x_ss, x_rs, z_ss, z_rs, b_ss, b_rs, know,
):
    rep, f = lax.axis_index("rep"), lax.axis_index("fsdp")
    zh, y = rep // NY, rep % NY
    zl, x, c = f // (2 * NX), (f // 2) % NX, f % 2
    z = zh * NL + zl

    def device(dx=0, dy=0, dl=0, dh=0, dc=0):
        to_rep = ((zh + dh) % NH) * NY + (y + dy) % NY
        to_f = (((zl + dl) % NL) * NX + (x + dx) % NX) * 2 + (c + dc) % 2
        return to_rep, to_f

    def signal(sem, **where):
        pl.semaphore_signal(sem, inc=1, device_id=device(**where), device_id_type=MESH)

    def prepare(src, dst, ss, rs, **where):
        return pltpu.make_async_remote_copy(
            src_ref=src, dst_ref=dst, send_sem=ss, recv_sem=rs, device_id=device(**where), device_id_type=MESH
        )

    def send(src, dst, ss, rs, **where):
        copy = prepare(src, dst, ss, rs, **where)
        copy.start()
        return copy

    barrier = pltpu.get_barrier_semaphore()
    signal(barrier, dc=1)
    for step in (1, 2, 3):
        signal(barrier, dx=step)
        signal(barrier, dy=step)
        signal(barrier, dl=step)

    @pl.when(zh == 0)
    def _():
        for step in (1, 2, 3):
            signal(barrier, dh=step)

    @pl.when((zh == 1) | (zh == 2))
    def _():
        signal(barrier, dh=1)

    @pl.when((zh == 2) | (zh == 3))
    def _():
        signal(barrier, dh=3)

    def pass_barrier():
        @pl.when(zh == 0)
        def _():
            pl.semaphore_wait(barrier, 10)

        @pl.when((zh == 1) | (zh == 3))
        def _():
            pl.semaphore_wait(barrier, 12)
            signal(know.at[0], dh=4 - zh)

        @pl.when(zh == 2)
        def _():
            pl.semaphore_wait(barrier, 13)
            signal(know.at[0], dh=2)
            signal(know.at[1], dh=1)
            signal(know.at[1], dh=3)

        for step in (1, 2, 3):
            signal(know.at[2], dx=step)

    loads = [
        pltpu.make_async_copy(grad_hbm.at[0, 0, pl.ds(r0, n)], grad.at[pl.ds(r0, n)], load_sem.at[k])
        for k, (r0, n) in enumerate(PIECES)
    ]
    extra = [
        pltpu.make_async_copy(src, dst, load_sem.at[K + i])
        for i, (src, dst) in enumerate(
            ((basis_hbm, basis_t), (rows_hbm, rows_t), (wide_hbm, wide_t), (mom_hbm.at[0], mom))
        )
    ]
    for copy in extra[:3] + loads + extra[3:]:
        copy.start()

    def columns(slot, dl, core):
        owner = (((zl + dl) % NL) * NX + (x + STEP_OF_SLOT[slot]) % NX) * 2 + core
        return pl.ds(pl.multiple_of(owner * WIDTH, WIDTH), WIDTH)

    def convert(k):
        r0, n = PIECES[k]
        for slot in range(4):
            for dl in range(NL):
                give[slot, dl, pl.ds(r0, n)] = grad[pl.ds(r0, n), columns(slot, dl, 1 - c)].astype(F32)

    def add_own(k, slot):
        r0, n = PIECES[k]
        for dl in range(NL):
            part[slot, dl, pl.ds(r0, n)] += grad[pl.ds(r0, n), columns(slot, dl, c)].astype(F32)

    sent = []
    core_far, core_rest = {}, {}

    def give_piece(k):
        r0, n = PIECES[k]
        rows = pl.ds(r0, n)
        core_far[k] = send(
            give.at[pl.ds(FAR, 1), :, rows], part.at[pl.ds(FAR, 1), :, rows], core_ss.at[2 * k], core_rs.at[2 * k], dc=1
        )
        core_rest[k] = send(
            give.at[pl.ds(1, 3), :, rows], part.at[pl.ds(1, 3), :, rows], core_ss.at[2 * k + 1], core_rs.at[2 * k + 1], dc=1
        )
        sent.extend((core_far[k], core_rest[k]))

    fars, nears, adds, zs = {}, {}, {}, {}

    def halves(k):
        r0, n = PIECES[k]
        return pl.ds(r0, n // 2), pl.ds(r0 + n // 2, n // 2), pl.ds(r0 // 2, n // 2)

    def open_piece(k):
        lower, upper, packed = halves(k)
        core_far[k].wait_recv()
        add_own(k, FAR)
        fars[k] = (
            send(part.at[FAR, :, lower], far_p.at[:, packed], x_ss.at[6 * k], x_rs.at[6 * k], dx=1),
            send(part.at[FAR, :, upper], far_m.at[:, packed], x_ss.at[6 * k + 1], x_rs.at[6 * k + 1], dx=-1),
        )
        core_rest[k].wait_recv()
        add_own(k, NEXT)
        add_own(k, PREV)
        nears[k] = (
            send(part.at[NEXT, :, upper], near_p.at[:, upper], x_ss.at[6 * k + 2], x_rs.at[6 * k + 2], dx=1),
            send(part.at[PREV, :, lower], near_m.at[:, lower], x_ss.at[6 * k + 3], x_rs.at[6 * k + 3], dx=-1),
        )
        add_own(k, OWN)
        sent.extend(fars[k] + nears[k])

    def pass_on(k):
        lower, upper, packed = halves(k)
        fars[k][0].wait_recv()
        part[NEXT, :, lower] += far_p[:, packed]
        first = send(part.at[NEXT, :, lower], near_p.at[:, lower], x_ss.at[6 * k + 4], x_rs.at[6 * k + 4], dx=1)
        fars[k][1].wait_recv()
        part[PREV, :, upper] += far_m[:, packed]
        second = send(part.at[PREV, :, upper], near_m.at[:, upper], x_ss.at[6 * k + 5], x_rs.at[6 * k + 5], dx=-1)
        adds[k] = (first, second)
        sent.extend(adds[k])

    def along_z(k):
        r0, n = PIECES[k]
        rows = pl.ds(r0, n)
        for copy in nears[k] + adds[k]:
            copy.wait_recv()
        zs[k] = []
        for dl in (3, 2, 1, 0):
            part[OWN, dl, rows] += near_p[dl, rows] + near_m[dl, rows]
            if dl:
                zs[k].append(
                    send(part.at[OWN, dl, rows], from_z.at[dl - 1, rows], z_ss.at[3 * k + dl - 1], z_rs.at[3 * k + dl - 1], dl=dl)
                )
        sent.extend(zs[k])

    def close(k):
        r0, n = PIECES[k]
        rows = pl.ds(r0, n)
        for copy in zs[k]:
            copy.wait_recv()
        out[0, rows] = rest[rows] + ((part[OWN, 0, rows] + from_z[0, rows]) + (from_z[1, rows] + from_z[2, rows]))

    def fold(left):
        high, low = split(jnp.concatenate([left[:8], left[8:]], axis=1))
        return jnp.concatenate([high, low], axis=0)

    def tile(both):
        return (both[:8, :128] + both[:8, 128:]) + both[8:, :128]

    def band_parts():
        step = 4
        for first in range(0, NL * NX * 2, step):
            left = dot(rows_t[...], grad[:, first * WIDTH : (first + step) * WIDTH])
            left = left[:16] + left[16:]
            for i in range(step):
                at = (first + i) * 16
                left_t[at : at + 16] = fold(left[:, i * WIDTH : (i + 1) * WIDTH])
        both = dot(left_t[...], wide_t[...])
        for owner in range(NL * NX * 2):
            which = (owner + c) % 2
            dl = (owner // (2 * NX) - zl + NL) % NL
            bands[which, dl, (owner // 2) % NX] = tile(both[owner * 16 : owner * 16 + 16])

    def band_of_momentum():
        high, low = split(mom[...])
        left = dot(rows_t[...], high)
        left = (left[:16] + left[16:]) + dot(rows_t[:16], low)
        return tile(dot(fold(left), wide_t[...]))

    def inverse(coeffs):
        high, low = split(coeffs)
        both = jnp.concatenate([high, low], axis=0)
        dims = (((1,), (1,)), ((), ()))
        one = lax.dot_general(both, wide_t[:, :128], dims, preferred_element_type=F32)
        two = lax.dot_general(both, wide_t[:, 128:], dims, preferred_element_type=F32)
        wide = (one[:8] + one[8:]) + two[:8]
        return [exact(basis_t[...], wide[:, i * WIDTH : (i + 1) * WIDTH], ((0,), (0,))) for i in range(2)]

    def band_core():
        copy = send(bands.at[1], bands_c, b_ss.at[0], b_rs.at[0], dc=1)
        sent.append(copy)
        return [copy]

    def band_z(copies):
        for copy in copies:
            copy.wait_recv()
        bands_c[...] += bands[0]
        copies = [send(bands_c.at[dl], bands_z.at[dl - 1], b_ss.at[dl], b_rs.at[dl], dl=dl) for dl in (2, 3, 1)]
        sent.extend(copies)
        return copies

    def band_xy(copies):
        for copy in copies:
            copy.wait_recv()
        sums_z[...] = (bands_c[0] + bands_z[0]) + (bands_z[1] + bands_z[2])
        sums_z[x] += 0.999 * band_of_momentum()
        bands_xy[y, 0] = sums_z[x]
        pl.semaphore_wait(know.at[2], 3)
        copies = []
        for dx in (2, 1, 3, 0):
            for dy in (2, 1, 3, 0):
                if dx or dy:
                    i = 4 + dx * 4 + dy
                    copies.append(send(sums_z.at[(x + dx) % NX], bands_xy.at[y, dx], b_ss.at[i], b_rs.at[i], dx=dx, dy=dy))
        sent.extend(copies)
        return copies

    def band_y(copies):
        for copy in copies:
            copy.wait_recv()
        for i in range(NY):
            sums_y[i] = (bands_xy[i, 0] + bands_xy[i, 1]) + (bands_xy[i, 2] + bands_xy[i, 3])
        bands_h[zh] = (sums_y[0] + sums_y[1]) + (sums_y[2] + sums_y[3])

    to_h = [None] + [prepare(bands_h.at[zh], bands_h.at[zh], b_ss.at[20 + dh], b_rs.at[20 + dh], dh=dh) for dh in (1, 2, 3)]

    def band_h():
        @pl.when(zh == 0)
        def _():
            pl.semaphore_wait(know.at[0], 3)

        to_h[1].start()
        to_h[3].start()

        @pl.when((zh == 1) | (zh == 3))
        def _():
            pl.semaphore_wait(know.at[1], 1)

        to_h[2].start()

    def find_rest():
        for i, value in enumerate(inverse(sums_y[y])):
            rows = pl.ds(i * GROUP, GROUP)
            rest[rows] = 0.999 * mom[rows] - value

    def band_end():
        for copy in to_h[1:]:
            copy.wait_recv()
        shared = ((bands_h[0] + bands_h[1]) + (bands_h[2] + bands_h[3])) * (1.0 / (NY * NH))
        for i, value in enumerate(inverse(shared)):
            out[1, pl.ds(i * GROUP, GROUP)] = value

    for copy in extra[:3] + loads:
        copy.wait()
    band_parts()
    convert(0)
    pass_barrier()
    b = band_core()
    give_piece(0)
    for k in range(1, K):
        convert(k)
        give_piece(k)
    extra[3].wait()
    b = band_z(b)
    open_piece(0)
    open_piece(1)
    pass_on(0)
    b = band_xy(b)
    open_piece(2)
    pass_on(1)
    open_piece(3)
    along_z(0)
    band_y(b)
    pl.when(zh > 0)(band_h)
    find_rest()
    pass_on(2)
    along_z(1)
    pass_on(3)
    along_z(2)
    close(0)
    pl.when(zh == 0)(band_h)
    along_z(3)
    close(1)
    close(2)
    close(3)
    band_end()
    for copy in sent + to_h[1:]:
        copy.wait_send()


def body(grad_parts, momentum):
    basis, rows, wide = tables()

    def halves(table, axis):
        high = table.astype(jnp.bfloat16)
        low = (table - high.astype(np.float32)).astype(jnp.bfloat16)
        return jnp.asarray(np.concatenate([high, low], axis=axis))

    operands = (grad_parts, momentum, jnp.asarray(basis), halves(rows, 0), halves(wide, 1))
    operands = [pltpu.with_memory_space_constraint(a, pltpu.HBM) for a in operands]
    vmem = pltpu.VMEM
    dma = pltpu.SemaphoreType.DMA
    tile = (8, 128)
    out = pl.pallas_call(
        kernel,
        out_shape=pltpu.VMEM((2, ROWS, WIDTH), F32),
        in_specs=[pl.BlockSpec(memory_space=pltpu.HBM)] * 5,
        out_specs=pl.BlockSpec(memory_space=pltpu.VMEM),
        scratch_shapes=[
            vmem((ROWS, 8192), BF16),
            vmem((ROWS, WIDTH), F32),
            vmem((BAND, GROUP), F32),
            vmem((32, ROWS), BF16),
            vmem((2 * WIDTH, 256), BF16),
            vmem((4, NL, ROWS, WIDTH), F32),
            vmem((4, NL, ROWS, WIDTH), F32),
            vmem((NL, ROWS // 2, WIDTH), F32),
            vmem((NL, ROWS // 2, WIDTH), F32),
            vmem((NL, ROWS, WIDTH), F32),
            vmem((NL, ROWS, WIDTH), F32),
            vmem((3, ROWS, WIDTH), F32),
            vmem((16 * NL * NX * 2, 2 * WIDTH), BF16),
            vmem((2, NL, NX, *tile), F32),
            vmem((NL, NX, *tile), F32),
            vmem((3, NX, *tile), F32),
            vmem((NX, *tile), F32),
            vmem((NY, NX, *tile), F32),
            vmem((NY, *tile), F32),
            vmem((NH, *tile), F32),
            vmem((ROWS, WIDTH), F32),
            dma((K + 4,)),
            dma((2 * K,)),
            dma((2 * K,)),
            dma((6 * K,)),
            dma((6 * K,)),
            dma((3 * K,)),
            dma((3 * K,)),
            dma((24,)),
            dma((24,)),
            pltpu.SemaphoreType.REGULAR((3,)),
        ],
        compiler_params=pltpu.CompilerParams(collective_id=0, has_side_effects=True, vmem_limit_bytes=56 * 2**20),
    )(*operands)
    return out[0][None], out[1]


def solution(mesh):
    in_specs = (P("rep", "fsdp", None, None), P("rep", None, "fsdp"))
    out_specs = (P("rep", None, "fsdp"), P(None, "fsdp"))
    return jax.shard_map(body, mesh=mesh, in_specs=in_specs, out_specs=out_specs, check_vma=False)
```

```python
import jax
import jax.numpy as jnp
import numpy as np
from jax import lax
from jax.experimental import pallas as pl
from jax.experimental.pallas import tpu as pltpu
from jax.sharding import PartitionSpec as P

MESH = pl.DeviceIdType.MESH
F32, BF16 = jnp.float32, jnp.bfloat16
GROUP, BAND = 64, 8
ROWS, WIDTH = 128, 256
NX = NY = NL = NH = 4

PIECES = ((0, 16), (16, 32), (48, 32), (80, 32), (112, 16))
Z_FIRST = (0,)
K = len(PIECES)
Z_ROWS = max(PIECES[k][0] + PIECES[k][1] for k in Z_FIRST)
FAR, NEXT, PREV, OWN = 0, 1, 2, 3
STEP_OF_SLOT = (2, 1, 3, 0)


def tables():
    freq = np.arange(BAND)[:, None]
    place = np.arange(GROUP)[None, :]
    scale = np.where(freq == 0, np.sqrt(1.0 / GROUP), np.sqrt(2.0 / GROUP))
    basis = (scale * np.cos(np.pi * (2 * place + 1) * freq / (2 * GROUP))).astype(np.float32)
    rows = np.kron(np.eye(ROWS // GROUP, dtype=np.float32), basis)
    cols = np.kron(np.eye(WIDTH // GROUP, dtype=np.float32), basis).T
    wide = np.zeros((2 * WIDTH, 128), np.float32)
    wide[:WIDTH, :32] = cols
    wide[WIDTH:, 32:64] = cols
    return basis, rows, wide


def split(value):
    high = value.astype(BF16)
    return high, (value - high.astype(F32)).astype(BF16)


def dot(a, b):
    return jnp.dot(a, b, preferred_element_type=F32)


def exact(a, b, dims):
    return lax.dot_general(a, b, (dims, ((), ())), precision=lax.Precision.HIGHEST, preferred_element_type=F32)


def kernel(
    grad_hbm, mom_hbm, basis_hbm, rows_hbm, wide_hbm, out, grad, mom, basis_t, rows_t, wide_t, give, part,
    far_p, far_m, near_p, near_m, from_z, all_z, left_t, bands, bands_c, bands_z, sums_z, bands_xy, sums_y, bands_h, rest,
    load_sem, core_ss, core_rs, x_ss, x_rs, z_ss, z_rs, b_ss, b_rs, know,
):
    rep, f = lax.axis_index("rep"), lax.axis_index("fsdp")
    zh, y = rep // NY, rep % NY
    zl, x, c = f // (2 * NX), (f // 2) % NX, f % 2
    z = zh * NL + zl

    def device(dx=0, dy=0, dl=0, dh=0, dc=0):
        to_rep = ((zh + dh + NH) % NH) * NY + (y + dy) % NY
        to_f = (((zl + dl) % NL) * NX + (x + dx) % NX) * 2 + (c + dc) % 2
        return to_rep, to_f

    def signal(sem, **where):
        pl.semaphore_signal(sem, inc=1, device_id=device(**where), device_id_type=MESH)

    def prepare(src, dst, ss, rs, **where):
        return pltpu.make_async_remote_copy(
            src_ref=src, dst_ref=dst, send_sem=ss, recv_sem=rs, device_id=device(**where), device_id_type=MESH
        )

    def send(src, dst, ss, rs, **where):
        copy = prepare(src, dst, ss, rs, **where)
        copy.start()
        return copy

    barrier = pltpu.get_barrier_semaphore()
    signal(barrier, dc=1)
    for step in (1, 2, 3):
        signal(barrier, dx=step)
        signal(barrier, dy=step)
        signal(barrier, dl=step)

    for step in (1, 2, 3):

        @pl.when(zh + step < NH)
        def _(step=step):
            signal(barrier, dh=step)

    @pl.when(zh == 3)
    def _():
        signal(barrier, dh=3)

    def pass_barrier():
        pl.semaphore_wait(barrier, 10 + zh + zh // 2 - zh // 3)
        for step in (1, 2, 3):

            @pl.when((zh >= step) & ((zh < 3) | (step > 1)))
            def _(step=step):
                signal(know.at[0], dh=-step)

        for step in (1, 2, 3):
            signal(know.at[2], dx=step)

    loads = [
        pltpu.make_async_copy(grad_hbm.at[0, 0, pl.ds(r0, n)], grad.at[pl.ds(r0, n)], load_sem.at[k])
        for k, (r0, n) in enumerate(PIECES)
    ]
    extra = [
        pltpu.make_async_copy(src, dst, load_sem.at[K + i])
        for i, (src, dst) in enumerate(
            ((basis_hbm, basis_t), (rows_hbm, rows_t), (wide_hbm, wide_t), (mom_hbm.at[0], mom))
        )
    ]
    for copy in extra[:3] + loads + extra[3:]:
        copy.start()

    def columns(slot, dl, core):
        owner = (((zl + dl) % NL) * NX + (x + STEP_OF_SLOT[slot]) % NX) * 2 + core
        return pl.ds(pl.multiple_of(owner * WIDTH, WIDTH), WIDTH)

    def convert(k):
        r0, n = PIECES[k]
        for slot in range(4):
            for dl in range(NL):
                give[slot, dl, pl.ds(r0, n)] = grad[pl.ds(r0, n), columns(slot, dl, 1 - c)].astype(F32)

    def add_own(k, slot):
        r0, n = PIECES[k]
        for dl in range(NL):
            part[slot, dl, pl.ds(r0, n)] += grad[pl.ds(r0, n), columns(slot, dl, c)].astype(F32)

    sent = []
    core_far, core_rest = {}, {}

    def give_piece(k):
        r0, n = PIECES[k]
        rows = pl.ds(r0, n)
        core_far[k] = send(
            give.at[pl.ds(FAR, 1), :, rows], part.at[pl.ds(FAR, 1), :, rows], core_ss.at[2 * k], core_rs.at[2 * k], dc=1
        )
        core_rest[k] = send(
            give.at[pl.ds(1, 3), :, rows], part.at[pl.ds(1, 3), :, rows], core_ss.at[2 * k + 1], core_rs.at[2 * k + 1], dc=1
        )
        sent.extend((core_far[k], core_rest[k]))

    fars, nears, adds, zs = {}, {}, {}, {}

    def halves(k):
        r0, n = PIECES[k]
        return pl.ds(r0, n // 2), pl.ds(r0 + n // 2, n // 2), pl.ds(r0 // 2, n // 2)

    def members(k):
        return pl.ds(0, 1 if k in Z_FIRST else NL)

    def send_far(k):
        lower, upper, packed = halves(k)
        dls = members(k)
        fars[k] = (
            send(part.at[FAR, dls, lower], far_p.at[dls, packed], x_ss.at[6 * k], x_rs.at[6 * k], dx=1),
            send(part.at[FAR, dls, upper], far_m.at[dls, packed], x_ss.at[6 * k + 1], x_rs.at[6 * k + 1], dx=-1),
        )
        sent.extend(fars[k])

    def send_near(k):
        lower, upper, packed = halves(k)
        dls = members(k)
        nears[k] = (
            send(part.at[NEXT, dls, upper], near_p.at[dls, upper], x_ss.at[6 * k + 2], x_rs.at[6 * k + 2], dx=1),
            send(part.at[PREV, dls, lower], near_m.at[dls, lower], x_ss.at[6 * k + 3], x_rs.at[6 * k + 3], dx=-1),
        )
        sent.extend(nears[k])

    def open_piece(k):
        core_far[k].wait_recv()
        add_own(k, FAR)
        send_far(k)
        core_rest[k].wait_recv()
        add_own(k, NEXT)
        add_own(k, PREV)
        send_near(k)
        add_own(k, OWN)

    def pass_on(k):
        lower, upper, packed = halves(k)
        dls = members(k)
        fars[k][0].wait_recv()
        part[NEXT, dls, lower] += far_p[dls, packed]
        first = send(part.at[NEXT, dls, lower], near_p.at[dls, lower], x_ss.at[6 * k + 4], x_rs.at[6 * k + 4], dx=1)
        fars[k][1].wait_recv()
        part[PREV, dls, upper] += far_m[dls, packed]
        second = send(part.at[PREV, dls, upper], near_m.at[dls, upper], x_ss.at[6 * k + 5], x_rs.at[6 * k + 5], dx=-1)
        adds[k] = (first, second)
        sent.extend(adds[k])

    def along_z(k):
        r0, n = PIECES[k]
        rows = pl.ds(r0, n)
        for copy in nears[k] + adds[k]:
            copy.wait_recv()
        zs[k] = []
        for dl in (3, 2, 1, 0):
            part[OWN, dl, rows] += near_p[dl, rows] + near_m[dl, rows]
            if dl:
                zs[k].append(
                    send(part.at[OWN, dl, rows], from_z.at[dl - 1, rows], z_ss.at[3 * k + dl - 1], z_rs.at[3 * k + dl - 1], dl=dl)
                )
        sent.extend(zs[k])

    def close(k):
        r0, n = PIECES[k]
        rows = pl.ds(r0, n)
        for copy in zs[k]:
            copy.wait_recv()
        out[0, rows] = rest[rows] + ((part[OWN, 0, rows] + from_z[0, rows]) + (from_z[1, rows] + from_z[2, rows]))

    def z_first(k):
        r0, n = PIECES[k]
        rows = pl.ds(r0, n)
        core_far[k].wait_recv()
        core_rest[k].wait_recv()
        for slot in range(4):
            add_own(k, slot)
        zs[k] = [
            send(part.at[:, dl, rows], all_z.at[dl - 1, :, rows], z_ss.at[3 * k + dl - 1], z_rs.at[3 * k + dl - 1], dl=dl)
            for dl in (3, 2, 1)
        ]
        sent.extend(zs[k])

    def x_second(k):
        r0, n = PIECES[k]
        rows = pl.ds(r0, n)
        for copy in zs[k]:
            copy.wait_recv()
        for slot in range(4):
            part[slot, 0, rows] += (all_z[0, slot, rows] + all_z[1, slot, rows]) + all_z[2, slot, rows]
            if slot == FAR:
                send_far(k)
        send_near(k)

    def close_x(k):
        r0, n = PIECES[k]
        rows = pl.ds(r0, n)
        for copy in nears[k] + adds[k]:
            copy.wait_recv()
        out[0, rows] = rest[rows] + (part[OWN, 0, rows] + (near_p[0, rows] + near_m[0, rows]))

    def fold(left):
        high, low = split(jnp.concatenate([left[:8], left[8:]], axis=1))
        return jnp.concatenate([high, low], axis=0)

    def tile(both):
        return (both[:8, :128] + both[:8, 128:]) + both[8:, :128]

    def band_parts():
        step = 4
        for first in range(0, NL * NX * 2, step):
            left = dot(rows_t[...], grad[:, first * WIDTH : (first + step) * WIDTH])
            left = left[:16] + left[16:]
            for i in range(step):
                at = (first + i) * 16
                left_t[at : at + 16] = fold(left[:, i * WIDTH : (i + 1) * WIDTH])
        both = dot(left_t[...], wide_t[...])
        for owner in range(NL * NX * 2):
            which = (owner + c) % 2
            dl = (owner // (2 * NX) - zl + NL) % NL
            bands[which, dl, (owner // 2) % NX] = tile(both[owner * 16 : owner * 16 + 16])

    def band_of_momentum():
        high, low = split(mom[...])
        left = dot(rows_t[...], high)
        left = (left[:16] + left[16:]) + dot(rows_t[:16], low)
        return tile(dot(fold(left), wide_t[...]))

    def inverse(coeffs):
        high, low = split(coeffs)
        both = jnp.concatenate([high, low], axis=0)
        dims = (((1,), (1,)), ((), ()))
        one = lax.dot_general(both, wide_t[:, :128], dims, preferred_element_type=F32)
        two = lax.dot_general(both, wide_t[:, 128:], dims, preferred_element_type=F32)
        wide = (one[:8] + one[8:]) + two[:8]
        return [exact(basis_t[...], wide[:, i * WIDTH : (i + 1) * WIDTH], ((0,), (0,))) for i in range(2)]

    def band_core():
        copy = send(bands.at[1], bands_c, b_ss.at[0], b_rs.at[0], dc=1)
        sent.append(copy)
        return [copy]

    def band_z(copies):
        for copy in copies:
            copy.wait_recv()
        bands_c[...] += bands[0]
        copies = [send(bands_c.at[dl], bands_z.at[dl - 1], b_ss.at[dl], b_rs.at[dl], dl=dl) for dl in (2, 3, 1)]
        sent.extend(copies)
        return copies

    def band_xy(copies):
        for copy in copies:
            copy.wait_recv()
        sums_z[...] = (bands_c[0] + bands_z[0]) + (bands_z[1] + bands_z[2])
        sums_z[x] += 0.999 * band_of_momentum()
        bands_xy[y, 0] = sums_z[x]
        pl.semaphore_wait(know.at[2], 3)
        copies = []
        for dx in (2, 1, 3, 0):
            for dy in (2, 1, 3, 0):
                if dx or dy:
                    i = 4 + dx * 4 + dy
                    copies.append(send(sums_z.at[(x + dx) % NX], bands_xy.at[y, dx], b_ss.at[i], b_rs.at[i], dx=dx, dy=dy))
        sent.extend(copies)
        return copies

    def band_y(copies):
        for copy in copies:
            copy.wait_recv()
        for i in range(NY):
            sums_y[i] = (bands_xy[i, 0] + bands_xy[i, 1]) + (bands_xy[i, 2] + bands_xy[i, 3])
        bands_h[zh] = (sums_y[0] + sums_y[1]) + (sums_y[2] + sums_y[3])

    to_h = [None] + [prepare(bands_h.at[zh], bands_h.at[zh], b_ss.at[20 + dh], b_rs.at[20 + dh], dh=dh) for dh in (1, 2, 3)]

    def band_h():
        @pl.when(zh == 0)
        def _():
            pl.semaphore_wait(know.at[0], 3)

        @pl.when(zh != 1)
        def _():
            for dh in (2, 1, 3):
                to_h[dh].start()

        @pl.when(zh == 1)
        def _():
            to_h[3].start()
            pl.semaphore_wait(know.at[0], 2)
            to_h[2].start()
            to_h[1].start()

    def find_rest():
        for i, value in enumerate(inverse(sums_y[y])):
            rows = pl.ds(i * GROUP, GROUP)
            rest[rows] = 0.999 * mom[rows] - value

    def band_end():
        for copy in to_h[1:]:
            copy.wait_recv()
        shared = ((bands_h[0] + bands_h[1]) + (bands_h[2] + bands_h[3])) * (1.0 / (NY * NH))
        for i, value in enumerate(inverse(shared)):
            out[1, pl.ds(i * GROUP, GROUP)] = value

    for copy in extra[:3] + loads:
        copy.wait()
    band_parts()
    convert(1)
    pass_barrier()
    b = band_core()
    give_piece(1)
    convert(0)
    give_piece(0)
    convert(2)
    give_piece(2)
    extra[3].wait()
    b = band_z(b)
    open_piece(1)
    z_first(0)
    convert(3)
    give_piece(3)
    open_piece(2)
    convert(4)
    give_piece(4)
    pass_on(1)
    b = band_xy(b)
    open_piece(3)
    pass_on(2)
    x_second(0)
    open_piece(4)
    along_z(1)
    band_y(b)
    pl.when(zh > 0)(band_h)
    find_rest()
    pass_on(3)
    pass_on(0)
    along_z(2)
    pass_on(4)
    along_z(3)
    close_x(0)
    close(1)
    pl.when(zh == 0)(band_h)
    close(2)
    along_z(4)
    close(3)
    close(4)
    band_end()
    for copy in sent + to_h[1:]:
        copy.wait_send()


def body(grad_parts, momentum):
    basis, rows, wide = tables()

    def halves(table, axis):
        high = table.astype(jnp.bfloat16)
        low = (table - high.astype(np.float32)).astype(jnp.bfloat16)
        return jnp.asarray(np.concatenate([high, low], axis=axis))

    operands = (grad_parts, momentum, jnp.asarray(basis), halves(rows, 0), halves(wide, 1))
    operands = [pltpu.with_memory_space_constraint(a, pltpu.HBM) for a in operands]
    vmem = pltpu.VMEM
    dma = pltpu.SemaphoreType.DMA
    tile = (8, 128)
    out = pl.pallas_call(
        kernel,
        out_shape=pltpu.VMEM((2, ROWS, WIDTH), F32),
        in_specs=[pl.BlockSpec(memory_space=pltpu.HBM)] * 5,
        out_specs=pl.BlockSpec(memory_space=pltpu.VMEM),
        scratch_shapes=[
            vmem((ROWS, 8192), BF16),
            vmem((ROWS, WIDTH), F32),
            vmem((BAND, GROUP), F32),
            vmem((32, ROWS), BF16),
            vmem((2 * WIDTH, 256), BF16),
            vmem((4, NL, ROWS, WIDTH), F32),
            vmem((4, NL, ROWS, WIDTH), F32),
            vmem((NL, ROWS // 2, WIDTH), F32),
            vmem((NL, ROWS // 2, WIDTH), F32),
            vmem((NL, ROWS, WIDTH), F32),
            vmem((NL, ROWS, WIDTH), F32),
            vmem((3, ROWS, WIDTH), F32),
            vmem((3, 4, Z_ROWS, WIDTH), F32),
            vmem((16 * NL * NX * 2, 2 * WIDTH), BF16),
            vmem((2, NL, NX, *tile), F32),
            vmem((NL, NX, *tile), F32),
            vmem((3, NX, *tile), F32),
            vmem((NX, *tile), F32),
            vmem((NY, NX, *tile), F32),
            vmem((NY, *tile), F32),
            vmem((NH, *tile), F32),
            vmem((ROWS, WIDTH), F32),
            dma((K + 4,)),
            dma((2 * K,)),
            dma((2 * K,)),
            dma((6 * K,)),
            dma((6 * K,)),
            dma((3 * K,)),
            dma((3 * K,)),
            dma((24,)),
            dma((24,)),
            pltpu.SemaphoreType.REGULAR((3,)),
        ],
        compiler_params=pltpu.CompilerParams(collective_id=0, has_side_effects=True, vmem_limit_bytes=56 * 2**20),
    )(*operands)
    return out[0][None], out[1]


def solution(mesh):
    in_specs = (P("rep", "fsdp", None, None), P("rep", None, "fsdp"))
    out_specs = (P("rep", None, "fsdp"), P(None, "fsdp"))
    return jax.shard_map(body, mesh=mesh, in_specs=in_specs, out_specs=out_specs, check_vma=False)
```

```python
import jax
import jax.numpy as jnp
import numpy as np
from jax import lax
from jax.experimental import pallas as pl
from jax.experimental.pallas import tpu as pltpu
from jax.sharding import PartitionSpec as P

MESH = pl.DeviceIdType.MESH
F32, BF16 = jnp.float32, jnp.bfloat16
GROUP, BAND = 64, 8
ROWS, WIDTH = 128, 256
NX = NY = NL = NH = 4

PIECES = ((0, 16), (16, 32), (48, 32), (80, 32), (112, 16))
Z_FIRST = (0,)
K = len(PIECES)
Z_ROWS = max(PIECES[k][0] + PIECES[k][1] for k in Z_FIRST)
FAR, NEXT, PREV, OWN = 0, 1, 2, 3
STEP_OF_SLOT = (2, 1, 3, 0)


def tables():
    freq = np.arange(BAND)[:, None]
    place = np.arange(GROUP)[None, :]
    scale = np.where(freq == 0, np.sqrt(1.0 / GROUP), np.sqrt(2.0 / GROUP))
    basis = (scale * np.cos(np.pi * (2 * place + 1) * freq / (2 * GROUP))).astype(np.float32)
    rows = np.kron(np.eye(ROWS // GROUP, dtype=np.float32), basis)
    cols = np.kron(np.eye(WIDTH // GROUP, dtype=np.float32), basis).T
    wide = np.zeros((2 * WIDTH, 128), np.float32)
    wide[:WIDTH, :32] = cols
    wide[WIDTH:, 32:64] = cols
    return basis, rows, wide


def split(value):
    high = value.astype(BF16)
    return high, (value - high.astype(F32)).astype(BF16)


def dot(a, b):
    return jnp.dot(a, b, preferred_element_type=F32)


def exact(a, b, dims):
    return lax.dot_general(a, b, (dims, ((), ())), precision=lax.Precision.HIGHEST, preferred_element_type=F32)


def kernel(
    grad_hbm, mom_hbm, basis_hbm, rows_hbm, wide_hbm, out, grad, mom, basis_t, rows_t, wide_t, give, part,
    far_p, far_m, near_p, near_m, from_z, all_z, left_t, bands, bands_c, bands_z, sums_z, bands_xy, sums_y, bands_h, rest,
    load_sem, core_ss, core_rs, x_ss, x_rs, z_ss, z_rs, b_ss, b_rs, know,
):
    rep, f = lax.axis_index("rep"), lax.axis_index("fsdp")
    zh, y = lax.div(rep, NY), lax.rem(rep, NY)
    zl, x, c = lax.div(f, 2 * NX), lax.rem(lax.div(f, 2), NX), lax.rem(f, 2)

    x_on = [2 * lax.rem(x + i, NX) for i in range(NX)]
    l_on = [2 * NX * lax.rem(zl + i, NL) for i in range(NL)]
    y_on = [lax.rem(y + i, NY) for i in range(NY)]
    h_on = [NY * lax.rem(zh + i, NH) for i in range(NH)]
    c_on = [c, 1 - c]

    def device(dx=0, dy=0, dl=0, dh=0, dc=0):
        return h_on[dh % NH] + y_on[dy % NY], l_on[dl % NL] + x_on[dx % NX] + c_on[dc]

    def signal(sem, **where):
        pl.semaphore_signal(sem, inc=1, device_id=device(**where), device_id_type=MESH)

    def prepare(src, dst, ss, rs, **where):
        return pltpu.make_async_remote_copy(
            src_ref=src, dst_ref=dst, send_sem=ss, recv_sem=rs, device_id=device(**where), device_id_type=MESH
        )

    def send(src, dst, ss, rs, **where):
        copy = prepare(src, dst, ss, rs, **where)
        copy.start()
        return copy

    barrier = pltpu.get_barrier_semaphore()
    for step in (3, 2, 1):
        signal(barrier, dl=step)
    for step in (2, 1, 3):
        signal(barrier, dx=step)
    for step in (2, 1, 3):
        signal(barrier, dy=step)
    signal(barrier, dc=1)

    for step in (1, 2, 3):

        @pl.when(zh + step < NH)
        def _(step=step):
            signal(barrier, dh=step)

    @pl.when(zh == 3)
    def _():
        signal(barrier, dh=3)

    def pass_barrier():
        pl.semaphore_wait(barrier, 10 + zh + lax.div(zh, 2) - lax.div(zh, 3))
        for step in (1, 2, 3):

            @pl.when((zh >= step) & ((zh < 3) | (step > 1)))
            def _(step=step):
                signal(know.at[0], dh=-step)

        for step in (1, 2, 3):
            signal(know.at[2], dx=step)

    loads = [
        pltpu.make_async_copy(grad_hbm.at[0, 0, pl.ds(r0, n)], grad.at[pl.ds(r0, n)], load_sem.at[k])
        for k, (r0, n) in enumerate(PIECES)
    ]
    extra = [
        pltpu.make_async_copy(src, dst, load_sem.at[K + i])
        for i, (src, dst) in enumerate(
            ((basis_hbm, basis_t), (rows_hbm, rows_t), (wide_hbm, wide_t), (mom_hbm.at[0], mom))
        )
    ]
    for copy in extra[:3] + loads + extra[3:]:
        copy.start()

    def columns(slot, dl, core):
        owner = l_on[dl] + x_on[STEP_OF_SLOT[slot]] + c_on[core]
        return pl.ds(pl.multiple_of(owner * WIDTH, WIDTH), WIDTH)

    def convert(k):
        r0, n = PIECES[k]
        for slot in range(4):
            for dl in range(NL):
                give[slot, dl, pl.ds(r0, n)] = grad[pl.ds(r0, n), columns(slot, dl, 1)].astype(F32)

    def add_own(k, slot):
        r0, n = PIECES[k]
        for dl in range(NL):
            part[slot, dl, pl.ds(r0, n)] += grad[pl.ds(r0, n), columns(slot, dl, 0)].astype(F32)

    sent = []

    def drain():
        while sent:
            sent.pop(0).wait_send()

    core_far, core_rest = {}, {}

    def give_piece(k):
        r0, n = PIECES[k]
        rows = pl.ds(r0, n)
        core_far[k] = send(
            give.at[pl.ds(FAR, 1), :, rows], part.at[pl.ds(FAR, 1), :, rows], core_ss.at[2 * k], core_rs.at[2 * k], dc=1
        )
        core_rest[k] = send(
            give.at[pl.ds(1, 3), :, rows], part.at[pl.ds(1, 3), :, rows], core_ss.at[2 * k + 1], core_rs.at[2 * k + 1], dc=1
        )
        sent.extend((core_far[k], core_rest[k]))

    fars, nears, adds, zs = {}, {}, {}, {}

    def halves(k):
        r0, n = PIECES[k]
        return pl.ds(r0, n // 2), pl.ds(r0 + n // 2, n // 2), pl.ds(r0 // 2, n // 2)

    def members(k):
        return pl.ds(0, 1 if k in Z_FIRST else NL)

    def send_far(k):
        lower, upper, packed = halves(k)
        dls = members(k)
        fars[k] = (
            send(part.at[FAR, dls, lower], far_p.at[dls, packed], x_ss.at[6 * k], x_rs.at[6 * k], dx=1),
            send(part.at[FAR, dls, upper], far_m.at[dls, packed], x_ss.at[6 * k + 1], x_rs.at[6 * k + 1], dx=-1),
        )
        sent.extend(fars[k])

    def send_near(k):
        lower, upper, packed = halves(k)
        dls = members(k)
        nears[k] = (
            send(part.at[NEXT, dls, upper], near_p.at[dls, upper], x_ss.at[6 * k + 2], x_rs.at[6 * k + 2], dx=1),
            send(part.at[PREV, dls, lower], near_m.at[dls, lower], x_ss.at[6 * k + 3], x_rs.at[6 * k + 3], dx=-1),
        )
        sent.extend(nears[k])

    def open_piece(k):
        core_far[k].wait_recv()
        add_own(k, FAR)
        send_far(k)
        core_rest[k].wait_recv()
        add_own(k, NEXT)
        add_own(k, PREV)
        send_near(k)
        add_own(k, OWN)

    def pass_on(k):
        lower, upper, packed = halves(k)
        dls = members(k)
        fars[k][0].wait_recv()
        part[NEXT, dls, lower] += far_p[dls, packed]
        first = send(part.at[NEXT, dls, lower], near_p.at[dls, lower], x_ss.at[6 * k + 4], x_rs.at[6 * k + 4], dx=1)
        fars[k][1].wait_recv()
        part[PREV, dls, upper] += far_m[dls, packed]
        second = send(part.at[PREV, dls, upper], near_m.at[dls, upper], x_ss.at[6 * k + 5], x_rs.at[6 * k + 5], dx=-1)
        adds[k] = (first, second)
        sent.extend(adds[k])

    def along_z(k):
        r0, n = PIECES[k]
        rows = pl.ds(r0, n)
        for copy in nears[k] + adds[k]:
            copy.wait_recv()
        zs[k] = []
        for dl in (3, 2, 1, 0):
            part[OWN, dl, rows] += near_p[dl, rows] + near_m[dl, rows]
            if dl:
                zs[k].append(
                    send(part.at[OWN, dl, rows], from_z.at[dl - 1, rows], z_ss.at[3 * k + dl - 1], z_rs.at[3 * k + dl - 1], dl=dl)
                )
        sent.extend(zs[k])

    def close(k):
        r0, n = PIECES[k]
        rows = pl.ds(r0, n)
        for copy in zs[k]:
            copy.wait_recv()
        out[0, rows] = rest[rows] + ((part[OWN, 0, rows] + from_z[0, rows]) + (from_z[1, rows] + from_z[2, rows]))

    def z_first(k):
        r0, n = PIECES[k]
        rows = pl.ds(r0, n)
        core_far[k].wait_recv()
        core_rest[k].wait_recv()
        for slot in range(4):
            add_own(k, slot)
        zs[k] = [
            send(part.at[:, dl, rows], all_z.at[dl - 1, :, rows], z_ss.at[3 * k + dl - 1], z_rs.at[3 * k + dl - 1], dl=dl)
            for dl in (3, 2, 1)
        ]
        sent.extend(zs[k])

    def x_second(k):
        r0, n = PIECES[k]
        rows = pl.ds(r0, n)
        for copy in zs[k]:
            copy.wait_recv()
        for slot in range(4):
            part[slot, 0, rows] += (all_z[0, slot, rows] + all_z[1, slot, rows]) + all_z[2, slot, rows]
            if slot == FAR:
                send_far(k)
        send_near(k)

    def close_x(k):
        r0, n = PIECES[k]
        rows = pl.ds(r0, n)
        for copy in nears[k] + adds[k]:
            copy.wait_recv()
        out[0, rows] = rest[rows] + (part[OWN, 0, rows] + (near_p[0, rows] + near_m[0, rows]))

    def fold(left):
        high, low = split(jnp.concatenate([left[:8], left[8:]], axis=1))
        return jnp.concatenate([high, low], axis=0)

    def tile(both):
        return (both[:8, :128] + both[:8, 128:]) + both[8:, :128]

    def band_parts():
        step = 4
        for first in range(0, NL * NX * 2, step):
            left = dot(rows_t[...], grad[:, first * WIDTH : (first + step) * WIDTH])
            left = left[:16] + left[16:]
            for i in range(step):
                at = (first + i) * 16
                left_t[at : at + 16] = fold(left[:, i * WIDTH : (i + 1) * WIDTH])
        both = dot(left_t[...], wide_t[...])
        for owner in range(NL * NX * 2):
            which = c_on[owner % 2]
            dl = lax.rem(owner // (2 * NX) - zl + NL, NL)
            bands[which, dl, owner // 2 % NX] = tile(both[owner * 16 : owner * 16 + 16])

    def band_of_momentum():
        high, low = split(mom[...])
        left = dot(rows_t[...], high)
        left = (left[:16] + left[16:]) + dot(rows_t[:16], low)
        return tile(dot(fold(left), wide_t[...]))

    def inverse(coeffs):
        high, low = split(coeffs)
        both = jnp.concatenate([high, low], axis=0)
        dims = (((1,), (1,)), ((), ()))
        one = lax.dot_general(both, wide_t[:, :128], dims, preferred_element_type=F32)
        two = lax.dot_general(both, wide_t[:, 128:], dims, preferred_element_type=F32)
        wide = (one[:8] + one[8:]) + two[:8]
        return [exact(basis_t[...], wide[:, i * WIDTH : (i + 1) * WIDTH], ((0,), (0,))) for i in range(2)]

    def band_core():
        copy = send(bands.at[1], bands_c, b_ss.at[0], b_rs.at[0], dc=1)
        sent.append(copy)
        return [copy]

    def band_z(copies):
        for copy in copies:
            copy.wait_recv()
        bands_c[...] += bands[0]
        copies = [send(bands_c.at[dl], bands_z.at[dl - 1], b_ss.at[dl], b_rs.at[dl], dl=dl) for dl in (2, 3, 1)]
        sent.extend(copies)
        return copies

    def band_xy(copies):
        for copy in copies:
            copy.wait_recv()
        sums_z[...] = (bands_c[0] + bands_z[0]) + (bands_z[1] + bands_z[2])
        sums_z[x] += 0.999 * band_of_momentum()
        bands_xy[y, 0] = sums_z[x]
        pl.semaphore_wait(know.at[2], 3)
        copies = []
        for dx in (2, 1, 3, 0):
            for dy in (2, 1, 3, 0):
                if dx or dy:
                    i = 4 + dx * 4 + dy
                    copies.append(send(sums_z.at[lax.div(x_on[dx], 2)], bands_xy.at[y, dx], b_ss.at[i], b_rs.at[i], dx=dx, dy=dy))
        sent.extend(copies)
        return copies

    def band_y(copies):
        for copy in copies:
            copy.wait_recv()
        for i in range(NY):
            sums_y[i] = (bands_xy[i, 0] + bands_xy[i, 1]) + (bands_xy[i, 2] + bands_xy[i, 3])
        bands_h[zh] = (sums_y[0] + sums_y[1]) + (sums_y[2] + sums_y[3])

    to_h = [None] + [prepare(bands_h.at[zh], bands_h.at[zh], b_ss.at[20 + dh], b_rs.at[20 + dh], dh=dh) for dh in (1, 2, 3)]

    def band_h(first):
        if first < 2:
            to_h[3].start() if first == 1 else None
            pl.semaphore_wait(know.at[0], 3 - first)
        for dh in (2, 1) if first == 1 else (2, 1, 3):
            to_h[dh].start()

    def find_rest():
        for i, value in enumerate(inverse(sums_y[y])):
            rows = pl.ds(i * GROUP, GROUP)
            rest[rows] = 0.999 * mom[rows] - value

    def band_end():
        for copy in to_h[1:]:
            copy.wait_recv()
        shared = ((bands_h[0] + bands_h[1]) + (bands_h[2] + bands_h[3])) * (1.0 / (NY * NH))
        for i, value in enumerate(inverse(shared)):
            out[1, pl.ds(i * GROUP, GROUP)] = value

    @pl.when(zh == 0)
    def _():
        for copy in extra[:3] + loads:
            copy.wait()
        convert(1)
        pass_barrier()
        give_piece(1)
        convert(2)
        give_piece(2)
        convert(0)
        give_piece(0)
        convert(3)
        give_piece(3)
        convert(4)
        give_piece(4)
        band_parts()
        b = band_core()
        extra[3].wait()
        open_piece(1)
        b = band_z(b)
        z_first(0)
        open_piece(2)
        pass_on(1)
        b = band_xy(b)
        open_piece(3)
        pass_on(2)
        open_piece(4)
        along_z(1)
        pass_on(3)
        x_second(0)
        along_z(2)
        band_y(b)
        find_rest()
        pass_on(4)
        pass_on(0)
        along_z(3)
        close(1)
        band_h(0)
        close(2)
        drain()
        along_z(4)
        close_x(0)
        close(3)
        band_end()
        close(4)
        drain()
        for copy in to_h[1:]:
            copy.wait_send()

    @pl.when(zh == 1)
    def _():
        for copy in extra[:3] + loads:
            copy.wait()
        band_parts()
        convert(1)
        pass_barrier()
        b = band_core()
        give_piece(1)
        convert(2)
        give_piece(2)
        extra[3].wait()
        b = band_z(b)
        open_piece(1)
        convert(0)
        give_piece(0)
        convert(3)
        give_piece(3)
        convert(4)
        give_piece(4)
        z_first(0)
        b = band_xy(b)
        open_piece(2)
        pass_on(1)
        open_piece(3)
        band_y(b)
        band_h(1)
        pass_on(2)
        find_rest()
        open_piece(4)
        along_z(1)
        pass_on(3)
        x_second(0)
        along_z(2)
        pass_on(4)
        pass_on(0)
        along_z(3)
        close(1)
        close(2)
        drain()
        along_z(4)
        close_x(0)
        close(3)
        band_end()
        close(4)
        drain()
        for copy in to_h[1:]:
            copy.wait_send()

    @pl.when(zh >= 2)
    def _():
        for copy in extra[:3] + loads:
            copy.wait()
        band_parts()
        convert(1)
        pass_barrier()
        b = band_core()
        give_piece(1)
        convert(2)
        give_piece(2)
        extra[3].wait()
        b = band_z(b)
        open_piece(1)
        convert(0)
        give_piece(0)
        convert(3)
        give_piece(3)
        convert(4)
        give_piece(4)
        z_first(0)
        b = band_xy(b)
        open_piece(2)
        pass_on(1)
        open_piece(3)
        band_y(b)
        band_h(2)
        pass_on(2)
        find_rest()
        open_piece(4)
        along_z(1)
        pass_on(3)
        x_second(0)
        along_z(2)
        pass_on(4)
        pass_on(0)
        along_z(3)
        close(1)
        close(2)
        drain()
        along_z(4)
        close_x(0)
        close(3)
        band_end()
        close(4)
        drain()
        for copy in to_h[1:]:
            copy.wait_send()


def body(grad_parts, momentum):
    basis, rows, wide = tables()

    def halves(table, axis):
        high = table.astype(jnp.bfloat16)
        low = (table - high.astype(np.float32)).astype(jnp.bfloat16)
        return jnp.asarray(np.concatenate([high, low], axis=axis))

    operands = (grad_parts, momentum, jnp.asarray(basis), halves(rows, 0), halves(wide, 1))
    operands = [pltpu.with_memory_space_constraint(a, pltpu.HBM) for a in operands]
    vmem = pltpu.VMEM
    dma = pltpu.SemaphoreType.DMA
    tile = (8, 128)
    out = pl.pallas_call(
        kernel,
        out_shape=pltpu.VMEM((2, ROWS, WIDTH), F32),
        in_specs=[pl.BlockSpec(memory_space=pltpu.HBM)] * 5,
        out_specs=pl.BlockSpec(memory_space=pltpu.VMEM),
        scratch_shapes=[
            vmem((ROWS, 8192), BF16),
            vmem((ROWS, WIDTH), F32),
            vmem((BAND, GROUP), F32),
            vmem((32, ROWS), BF16),
            vmem((2 * WIDTH, 256), BF16),
            vmem((4, NL, ROWS, WIDTH), F32),
            vmem((4, NL, ROWS, WIDTH), F32),
            vmem((NL, ROWS // 2, WIDTH), F32),
            vmem((NL, ROWS // 2, WIDTH), F32),
            vmem((NL, ROWS, WIDTH), F32),
            vmem((NL, ROWS, WIDTH), F32),
            vmem((3, ROWS, WIDTH), F32),
            vmem((3, 4, Z_ROWS, WIDTH), F32),
            vmem((16 * NL * NX * 2, 2 * WIDTH), BF16),
            vmem((2, NL, NX, *tile), F32),
            vmem((NL, NX, *tile), F32),
            vmem((3, NX, *tile), F32),
            vmem((NX, *tile), F32),
            vmem((NY, NX, *tile), F32),
            vmem((NY, *tile), F32),
            vmem((NH, *tile), F32),
            vmem((ROWS, WIDTH), F32),
            dma((K + 4,)),
            dma((2 * K,)),
            dma((2 * K,)),
            dma((6 * K,)),
            dma((6 * K,)),
            dma((3 * K,)),
            dma((3 * K,)),
            dma((24,)),
            dma((24,)),
            pltpu.SemaphoreType.REGULAR((3,)),
        ],
        compiler_params=pltpu.CompilerParams(collective_id=0, has_side_effects=True, vmem_limit_bytes=56 * 2**20),
    )(*operands)
    return out[0][None], out[1]


def solution(mesh):
    in_specs = (P("rep", "fsdp", None, None), P("rep", None, "fsdp"))
    out_specs = (P("rep", None, "fsdp"), P(None, "fsdp"))
    return jax.shard_map(body, mesh=mesh, in_specs=in_specs, out_specs=out_specs, check_vma=False)
```

```python
import jax
import jax.numpy as jnp
import numpy as np
from jax import lax
from jax.experimental import pallas as pl
from jax.experimental.pallas import tpu as pltpu
from jax.sharding import PartitionSpec as P

MESH = pl.DeviceIdType.MESH
F32, BF16 = jnp.float32, jnp.bfloat16
GROUP, BAND = 64, 8
ROWS, WIDTH = 128, 256
NX = NY = NL = NH = 4

PIECES = ((0, 16), (16, 32), (48, 32), (80, 32), (112, 16))
Z_FIRST = (0,)
K = len(PIECES)
Z_ROWS = max(PIECES[k][0] + PIECES[k][1] for k in Z_FIRST)
FAR, NEXT, PREV, OWN = 0, 1, 2, 3
STEP_OF_SLOT = (2, 1, 3, 0)


def tables():
    freq = np.arange(BAND)[:, None]
    place = np.arange(GROUP)[None, :]
    scale = np.where(freq == 0, np.sqrt(1.0 / GROUP), np.sqrt(2.0 / GROUP))
    basis = (scale * np.cos(np.pi * (2 * place + 1) * freq / (2 * GROUP))).astype(np.float32)
    rows = np.kron(np.eye(ROWS // GROUP, dtype=np.float32), basis)
    cols = np.kron(np.eye(WIDTH // GROUP, dtype=np.float32), basis).T
    wide = np.zeros((2 * WIDTH, 128), np.float32)
    wide[:WIDTH, :32] = cols
    wide[WIDTH:, 32:64] = cols
    return basis, rows, wide


def split(value):
    high = value.astype(BF16)
    return high, (value - high.astype(F32)).astype(BF16)


def dot(a, b):
    return jnp.dot(a, b, preferred_element_type=F32)


def exact(a, b, dims):
    return lax.dot_general(a, b, (dims, ((), ())), precision=lax.Precision.HIGHEST, preferred_element_type=F32)


def kernel(
    grad_hbm, mom_hbm, basis_hbm, rows_hbm, wide_hbm, out, grad, mom, basis_t, rows_t, wide_t, give, part,
    far_p, far_m, near_p, near_m, from_z, all_z, left_t, bands, bands_c, bands_z, sums_z, bands_xy, sums_y, bands_h, rest,
    load_sem, core_ss, core_rs, x_ss, x_rs, z_ss, z_rs, b_ss, b_rs, know,
):
    rep, f = lax.axis_index("rep"), lax.axis_index("fsdp")
    zh, y = lax.div(rep, NY), lax.rem(rep, NY)
    zl, x, c = lax.div(f, 2 * NX), lax.rem(lax.div(f, 2), NX), lax.rem(f, 2)

    x_on = [2 * lax.rem(x + i, NX) for i in range(NX)]
    l_on = [2 * NX * lax.rem(zl + i, NL) for i in range(NL)]
    y_on = [lax.rem(y + i, NY) for i in range(NY)]
    h_on = [NY * lax.rem(zh + i, NH) for i in range(NH)]
    c_on = [c, 1 - c]

    def device(dx=0, dy=0, dl=0, dh=0, dc=0):
        return h_on[dh % NH] + y_on[dy % NY], l_on[dl % NL] + x_on[dx % NX] + c_on[dc]

    def signal(sem, **where):
        pl.semaphore_signal(sem, inc=1, device_id=device(**where), device_id_type=MESH)

    def prepare(src, dst, ss, rs, **where):
        return pltpu.make_async_remote_copy(
            src_ref=src, dst_ref=dst, send_sem=ss, recv_sem=rs, device_id=device(**where), device_id_type=MESH
        )

    def send(src, dst, ss, rs, **where):
        copy = prepare(src, dst, ss, rs, **where)
        copy.start()
        return copy

    barrier = pltpu.get_barrier_semaphore()
    inner = (zl == 1) | (zl == 2)
    late = zh >= 2
    edge = ((zh == 2) & (zl == 3)) | ((zh == 3) & (zl == 0))

    @pl.when(late)
    def _():
        for step in (3, 2, 1):
            signal(barrier, dl=step)
        for step in (2, 1, 3):
            signal(barrier, dx=step)
        for step in (2, 1, 3):
            signal(barrier, dy=step)

    @pl.when(jnp.logical_not(late))
    def _():
        for step in (1, 3):
            signal(barrier, dx=step)
            signal(barrier, dy=step)

        @pl.when(zl < 3)
        def _():
            signal(barrier, dl=1)

        @pl.when(zl > 0)
        def _():
            signal(barrier, dl=3)

    signal(barrier, dc=1)

    @pl.when(zh == 0)
    def _():
        for step in (1, 2, 3):
            signal(barrier, dh=step)

    @pl.when(zh == 1)
    def _():
        for step in (1, 2):
            signal(barrier, dh=step)

    def meet(sem):
        @pl.when((zh == 2) & (zl == 3))
        def _():
            signal(sem, dh=1, dl=1)

        @pl.when((zh == 3) & (zl == 0))
        def _():
            signal(sem, dh=3, dl=3)

    meet(barrier)

    def pass_barrier(early):
        if early:
            pl.semaphore_wait(barrier, 6 + lax.rem(lax.div(zl + 1, 2), 2) + zh)
            signal(know.at[3], dx=1)
            signal(know.at[4], dy=1)

            @pl.when(inner)
            def _():
                signal(know.at[5], dl=1)
                signal(know.at[5], dl=3)

        else:
            pl.semaphore_wait(barrier, 12 + jnp.where(edge, 1, 0))
            meet(know.at[3])
            tell_y()
        for step in (1, 2, 3):

            @pl.when((zh >= step) & ((zh < 3) | (step > 1)))
            def _(step=step):
                signal(know.at[0], dh=-step)

    def tell_y():
        for step in (1, 2, 3):
            signal(know.at[2], dx=step)

    def learn_xy():
        pl.semaphore_wait(know.at[3], 1)
        pl.semaphore_wait(know.at[4], 1)
        tell_y()

    def learn_z():
        pl.semaphore_wait(know.at[5], 1)

        @pl.when(zl == 1)
        def _():
            signal(know.at[6], dl=3)

        @pl.when(zl == 2)
        def _():
            signal(know.at[6], dl=1)

        @pl.when(jnp.logical_not(inner))
        def _():
            pl.semaphore_wait(know.at[6], 1)

    def pass_meeting():
        @pl.when(edge)
        def _():
            pl.semaphore_wait(know.at[3], 1)
            for step in (1, 2, 3):
                signal(know.at[4], dl=step)

    def learn_meeting():
        @pl.when(jnp.logical_not(edge))
        def _():
            pl.semaphore_wait(know.at[4], 1)

    loads = [
        pltpu.make_async_copy(grad_hbm.at[0, 0, pl.ds(r0, n)], grad.at[pl.ds(r0, n)], load_sem.at[k])
        for k, (r0, n) in enumerate(PIECES)
    ]
    extra = [
        pltpu.make_async_copy(src, dst, load_sem.at[K + i])
        for i, (src, dst) in enumerate(
            ((basis_hbm, basis_t), (rows_hbm, rows_t), (wide_hbm, wide_t), (mom_hbm.at[0], mom))
        )
    ]
    for copy in [loads[1]] + extra[:3] + [loads[2], loads[0]] + loads[3:] + extra[3:]:
        copy.start()

    def columns(slot, dl, core):
        owner = l_on[dl] + x_on[STEP_OF_SLOT[slot]] + c_on[core]
        return pl.ds(pl.multiple_of(owner * WIDTH, WIDTH), WIDTH)

    def convert(k):
        r0, n = PIECES[k]
        for slot in range(4):
            for dl in range(NL):
                give[slot, dl, pl.ds(r0, n)] = grad[pl.ds(r0, n), columns(slot, dl, 1)].astype(F32)

    def add_own(k, slot):
        r0, n = PIECES[k]
        for dl in range(NL):
            part[slot, dl, pl.ds(r0, n)] += grad[pl.ds(r0, n), columns(slot, dl, 0)].astype(F32)

    sent = []

    def drain():
        while sent:
            sent.pop(0).wait_send()

    core_far, core_rest = {}, {}

    def give_piece(k):
        r0, n = PIECES[k]
        rows = pl.ds(r0, n)
        core_far[k] = send(
            give.at[pl.ds(FAR, 1), :, rows], part.at[pl.ds(FAR, 1), :, rows], core_ss.at[2 * k], core_rs.at[2 * k], dc=1
        )
        core_rest[k] = send(
            give.at[pl.ds(1, 3), :, rows], part.at[pl.ds(1, 3), :, rows], core_ss.at[2 * k + 1], core_rs.at[2 * k + 1], dc=1
        )
        sent.extend((core_far[k], core_rest[k]))

    fars, nears, adds, zs = {}, {}, {}, {}

    def halves(k):
        r0, n = PIECES[k]
        return pl.ds(r0, n // 2), pl.ds(r0 + n // 2, n // 2), pl.ds(r0 // 2, n // 2)

    def members(k):
        return pl.ds(0, 1 if k in Z_FIRST else NL)

    def send_far(k):
        lower, upper, packed = halves(k)
        dls = members(k)
        fars[k] = (
            send(part.at[FAR, dls, lower], far_p.at[dls, packed], x_ss.at[6 * k], x_rs.at[6 * k], dx=1),
            send(part.at[FAR, dls, upper], far_m.at[dls, packed], x_ss.at[6 * k + 1], x_rs.at[6 * k + 1], dx=-1),
        )
        sent.extend(fars[k])

    def send_near(k):
        lower, upper, packed = halves(k)
        dls = members(k)
        nears[k] = (
            send(part.at[NEXT, dls, upper], near_p.at[dls, upper], x_ss.at[6 * k + 2], x_rs.at[6 * k + 2], dx=1),
            send(part.at[PREV, dls, lower], near_m.at[dls, lower], x_ss.at[6 * k + 3], x_rs.at[6 * k + 3], dx=-1),
        )
        sent.extend(nears[k])

    def open_piece(k):
        core_far[k].wait_recv()
        add_own(k, FAR)
        send_far(k)
        core_rest[k].wait_recv()
        add_own(k, NEXT)
        add_own(k, PREV)
        send_near(k)
        add_own(k, OWN)

    def pass_on(k):
        lower, upper, packed = halves(k)
        dls = members(k)
        fars[k][0].wait_recv()
        part[NEXT, dls, lower] += far_p[dls, packed]
        first = send(part.at[NEXT, dls, lower], near_p.at[dls, lower], x_ss.at[6 * k + 4], x_rs.at[6 * k + 4], dx=1)
        fars[k][1].wait_recv()
        part[PREV, dls, upper] += far_m[dls, packed]
        second = send(part.at[PREV, dls, upper], near_m.at[dls, upper], x_ss.at[6 * k + 5], x_rs.at[6 * k + 5], dx=-1)
        adds[k] = (first, second)
        sent.extend(adds[k])

    def along_z(k):
        r0, n = PIECES[k]
        rows = pl.ds(r0, n)
        for copy in nears[k] + adds[k]:
            copy.wait_recv()
        zs[k] = []
        for dl in (3, 2, 1, 0):
            part[OWN, dl, rows] += near_p[dl, rows] + near_m[dl, rows]
            if dl:
                zs[k].append(
                    send(part.at[OWN, dl, rows], from_z.at[dl - 1, rows], z_ss.at[3 * k + dl - 1], z_rs.at[3 * k + dl - 1], dl=dl)
                )
        sent.extend(zs[k])

    def close(k):
        r0, n = PIECES[k]
        rows = pl.ds(r0, n)
        for copy in zs[k]:
            copy.wait_recv()
        out[0, rows] = rest[rows] + ((part[OWN, 0, rows] + from_z[0, rows]) + (from_z[1, rows] + from_z[2, rows]))

    def z_first(k):
        r0, n = PIECES[k]
        rows = pl.ds(r0, n)
        core_far[k].wait_recv()
        core_rest[k].wait_recv()
        for slot in range(4):
            add_own(k, slot)
        zs[k] = [
            send(part.at[:, dl, rows], all_z.at[dl - 1, :, rows], z_ss.at[3 * k + dl - 1], z_rs.at[3 * k + dl - 1], dl=dl)
            for dl in (3, 2, 1)
        ]
        sent.extend(zs[k])

    def x_second(k):
        r0, n = PIECES[k]
        rows = pl.ds(r0, n)
        for copy in zs[k]:
            copy.wait_recv()
        for slot in range(4):
            part[slot, 0, rows] += (all_z[0, slot, rows] + all_z[1, slot, rows]) + all_z[2, slot, rows]
            if slot == FAR:
                send_far(k)
        send_near(k)

    def close_x(k):
        r0, n = PIECES[k]
        rows = pl.ds(r0, n)
        for copy in nears[k] + adds[k]:
            copy.wait_recv()
        out[0, rows] = rest[rows] + (part[OWN, 0, rows] + (near_p[0, rows] + near_m[0, rows]))

    def fold(left):
        high, low = split(jnp.concatenate([left[:8], left[8:]], axis=1))
        return jnp.concatenate([high, low], axis=0)

    def tile(both):
        return (both[:8, :128] + both[:8, 128:]) + both[8:, :128]

    def band_parts():
        step = 4
        for first in range(0, NL * NX * 2, step):
            left = dot(rows_t[...], grad[:, first * WIDTH : (first + step) * WIDTH])
            left = left[:16] + left[16:]
            for i in range(step):
                at = (first + i) * 16
                left_t[at : at + 16] = fold(left[:, i * WIDTH : (i + 1) * WIDTH])
        both = dot(left_t[...], wide_t[...])
        for owner in range(NL * NX * 2):
            which = c_on[owner % 2]
            dl = lax.rem(owner // (2 * NX) - zl + NL, NL)
            bands[which, dl, owner // 2 % NX] = tile(both[owner * 16 : owner * 16 + 16])

    def band_of_momentum():
        high, low = split(mom[...])
        left = dot(rows_t[...], high)
        left = (left[:16] + left[16:]) + dot(rows_t[:16], low)
        return tile(dot(fold(left), wide_t[...]))

    def inverse(coeffs):
        high, low = split(coeffs)
        both = jnp.concatenate([high, low], axis=0)
        dims = (((1,), (1,)), ((), ()))
        one = lax.dot_general(both, wide_t[:, :128], dims, preferred_element_type=F32)
        two = lax.dot_general(both, wide_t[:, 128:], dims, preferred_element_type=F32)
        wide = (one[:8] + one[8:]) + two[:8]
        return [exact(basis_t[...], wide[:, i * WIDTH : (i + 1) * WIDTH], ((0,), (0,))) for i in range(2)]

    def band_core():
        copy = send(bands.at[1], bands_c, b_ss.at[0], b_rs.at[0], dc=1)
        sent.append(copy)
        return [copy]

    def band_z(copies):
        for copy in copies:
            copy.wait_recv()
        bands_c[...] += bands[0]
        copies = [send(bands_c.at[dl], bands_z.at[dl - 1], b_ss.at[dl], b_rs.at[dl], dl=dl) for dl in (2, 3, 1)]
        sent.extend(copies)
        return copies

    def band_xy(copies):
        for copy in copies:
            copy.wait_recv()
        sums_z[...] = (bands_c[0] + bands_z[0]) + (bands_z[1] + bands_z[2])
        sums_z[x] += 0.999 * band_of_momentum()
        bands_xy[y, 0] = sums_z[x]
        pl.semaphore_wait(know.at[2], 3)
        copies = []
        for dx in (2, 1, 3, 0):
            for dy in (2, 1, 3, 0):
                if dx or dy:
                    i = 4 + dx * 4 + dy
                    copies.append(send(sums_z.at[lax.div(x_on[dx], 2)], bands_xy.at[y, dx], b_ss.at[i], b_rs.at[i], dx=dx, dy=dy))
        sent.extend(copies)
        return copies

    def band_y(copies):
        for copy in copies:
            copy.wait_recv()
        for i in range(NY):
            sums_y[i] = (bands_xy[i, 0] + bands_xy[i, 1]) + (bands_xy[i, 2] + bands_xy[i, 3])
        bands_h[zh] = (sums_y[0] + sums_y[1]) + (sums_y[2] + sums_y[3])

    to_h = [None] + [prepare(bands_h.at[zh], bands_h.at[zh], b_ss.at[20 + dh], b_rs.at[20 + dh], dh=dh) for dh in (1, 2, 3)]

    def band_h(first):
        if first == 1:
            to_h[3].start()
        if first < 2:
            pl.semaphore_wait(know.at[0], 3 - first)
        else:
            learn_meeting()
        for dh in (2, 1) if first == 1 else (2, 1, 3):
            to_h[dh].start()

    def find_rest():
        for i, value in enumerate(inverse(sums_y[y])):
            rows = pl.ds(i * GROUP, GROUP)
            rest[rows] = 0.999 * mom[rows] - value

    def band_end():
        for copy in to_h[1:]:
            copy.wait_recv()
        shared = ((bands_h[0] + bands_h[1]) + (bands_h[2] + bands_h[3])) * (1.0 / (NY * NH))
        for i, value in enumerate(inverse(shared)):
            out[1, pl.ds(i * GROUP, GROUP)] = value

    @pl.when(zh == 0)
    def _():
        loads[1].wait()
        convert(1)
        pass_barrier(True)
        give_piece(1)
        for copy in extra[:3] + loads[:1] + loads[2:]:
            copy.wait()
        convert(2)
        give_piece(2)
        convert(0)
        give_piece(0)
        convert(3)
        give_piece(3)
        convert(4)
        give_piece(4)
        open_piece(1)
        learn_xy()
        open_piece(2)
        learn_z()
        z_first(0)
        band_parts()
        b = band_core()
        pass_on(1)
        extra[3].wait()
        b = band_z(b)
        open_piece(3)
        pass_on(2)
        open_piece(4)
        along_z(1)
        pass_on(3)
        b = band_xy(b)
        x_second(0)
        along_z(2)
        pass_on(4)
        pass_on(0)
        along_z(3)
        band_y(b)
        find_rest()
        close(1)
        band_h(0)
        close(2)
        drain()
        along_z(4)
        close_x(0)
        close(3)
        band_end()
        close(4)
        drain()
        for copy in to_h[1:]:
            copy.wait_send()

    @pl.when(zh == 1)
    def _():
        loads[1].wait()
        convert(1)
        pass_barrier(True)
        give_piece(1)
        for copy in extra[:3] + loads[:1] + loads[2:]:
            copy.wait()
        convert(2)
        give_piece(2)
        band_parts()
        b = band_core()
        extra[3].wait()
        open_piece(1)
        learn_xy()
        convert(0)
        give_piece(0)
        convert(3)
        give_piece(3)
        convert(4)
        give_piece(4)
        open_piece(2)
        learn_z()
        b = band_z(b)
        z_first(0)
        b = band_xy(b)
        pass_on(1)
        open_piece(3)
        band_y(b)
        band_h(1)
        pass_on(2)
        find_rest()
        open_piece(4)
        along_z(1)
        pass_on(3)
        x_second(0)
        along_z(2)
        pass_on(4)
        pass_on(0)
        along_z(3)
        close(1)
        close(2)
        drain()
        along_z(4)
        close_x(0)
        close(3)
        band_end()
        close(4)
        drain()
        for copy in to_h[1:]:
            copy.wait_send()

    @pl.when(zh >= 2)
    def _():
        loads[1].wait()
        for copy in extra[:3] + loads[:1] + loads[2:]:
            copy.wait()
        band_parts()
        convert(1)
        pass_barrier(False)
        b = band_core()
        give_piece(1)
        convert(2)
        give_piece(2)
        extra[3].wait()
        b = band_z(b)
        open_piece(1)
        pass_meeting()
        convert(0)
        give_piece(0)
        convert(3)
        give_piece(3)
        convert(4)
        give_piece(4)
        z_first(0)
        b = band_xy(b)
        open_piece(2)
        pass_on(1)
        open_piece(3)
        band_y(b)
        band_h(2)
        pass_on(2)
        find_rest()
        open_piece(4)
        along_z(1)
        pass_on(3)
        x_second(0)
        along_z(2)
        pass_on(4)
        pass_on(0)
        along_z(3)
        close(1)
        close(2)
        drain()
        along_z(4)
        close_x(0)
        close(3)
        band_end()
        close(4)
        drain()
        for copy in to_h[1:]:
            copy.wait_send()


def body(grad_parts, momentum):
    basis, rows, wide = tables()

    def halves(table, axis):
        high = table.astype(jnp.bfloat16)
        low = (table - high.astype(np.float32)).astype(jnp.bfloat16)
        return jnp.asarray(np.concatenate([high, low], axis=axis))

    operands = (grad_parts, momentum, jnp.asarray(basis), halves(rows, 0), halves(wide, 1))
    operands = [pltpu.with_memory_space_constraint(a, pltpu.HBM) for a in operands]
    vmem = pltpu.VMEM
    dma = pltpu.SemaphoreType.DMA
    tile = (8, 128)
    out = pl.pallas_call(
        kernel,
        out_shape=pltpu.VMEM((2, ROWS, WIDTH), F32),
        in_specs=[pl.BlockSpec(memory_space=pltpu.HBM)] * 5,
        out_specs=pl.BlockSpec(memory_space=pltpu.VMEM),
        scratch_shapes=[
            vmem((ROWS, 8192), BF16),
            vmem((ROWS, WIDTH), F32),
            vmem((BAND, GROUP), F32),
            vmem((32, ROWS), BF16),
            vmem((2 * WIDTH, 256), BF16),
            vmem((4, NL, ROWS, WIDTH), F32),
            vmem((4, NL, ROWS, WIDTH), F32),
            vmem((NL, ROWS // 2, WIDTH), F32),
            vmem((NL, ROWS // 2, WIDTH), F32),
            vmem((NL, ROWS, WIDTH), F32),
            vmem((NL, ROWS, WIDTH), F32),
            vmem((3, ROWS, WIDTH), F32),
            vmem((3, 4, Z_ROWS, WIDTH), F32),
            vmem((16 * NL * NX * 2, 2 * WIDTH), BF16),
            vmem((2, NL, NX, *tile), F32),
            vmem((NL, NX, *tile), F32),
            vmem((3, NX, *tile), F32),
            vmem((NX, *tile), F32),
            vmem((NY, NX, *tile), F32),
            vmem((NY, *tile), F32),
            vmem((NH, *tile), F32),
            vmem((ROWS, WIDTH), F32),
            dma((K + 4,)),
            dma((2 * K,)),
            dma((2 * K,)),
            dma((6 * K,)),
            dma((6 * K,)),
            dma((3 * K,)),
            dma((3 * K,)),
            dma((24,)),
            dma((24,)),
            pltpu.SemaphoreType.REGULAR((7,)),
        ],
        compiler_params=pltpu.CompilerParams(collective_id=0, has_side_effects=True, vmem_limit_bytes=56 * 2**20),
    )(*operands)
    return out[0][None], out[1]


def solution(mesh):
    in_specs = (P("rep", "fsdp", None, None), P("rep", None, "fsdp"))
    out_specs = (P("rep", None, "fsdp"), P(None, "fsdp"))
    return jax.shard_map(body, mesh=mesh, in_specs=in_specs, out_specs=out_specs, check_vma=False)
```

```python
import jax
import jax.numpy as jnp
import numpy as np
from jax import lax
from jax.experimental import pallas as pl
from jax.experimental.pallas import tpu as pltpu
from jax.sharding import PartitionSpec as P

MESH = pl.DeviceIdType.MESH
F32, BF16 = jnp.float32, jnp.bfloat16
GROUP, BAND = 64, 8
ROWS, WIDTH = 128, 256
NX = NY = NL = NH = 4

PIECES = ((0, 16), (16, 32), (48, 32), (80, 32), (112, 16))
Z_FIRST = (0,)
K = len(PIECES)
Z_ROWS = max(PIECES[k][0] + PIECES[k][1] for k in Z_FIRST)
FAR, NEXT, PREV, OWN = 0, 1, 2, 3
STEP_OF_SLOT = (2, 1, 3, 0)


def tables():
    freq = np.arange(BAND)[:, None]
    place = np.arange(GROUP)[None, :]
    scale = np.where(freq == 0, np.sqrt(1.0 / GROUP), np.sqrt(2.0 / GROUP))
    basis = (scale * np.cos(np.pi * (2 * place + 1) * freq / (2 * GROUP))).astype(np.float32)
    rows = np.kron(np.eye(ROWS // GROUP, dtype=np.float32), basis)
    cols = np.kron(np.eye(WIDTH // GROUP, dtype=np.float32), basis).T
    wide = np.zeros((2 * WIDTH, 128), np.float32)
    wide[:WIDTH, :32] = cols
    wide[WIDTH:, 32:64] = cols
    return basis, rows, wide


def split(value):
    high = value.astype(BF16)
    return high, (value - high.astype(F32)).astype(BF16)


def dot(a, b):
    return jnp.dot(a, b, preferred_element_type=F32)


def exact(a, b, dims):
    return lax.dot_general(a, b, (dims, ((), ())), precision=lax.Precision.HIGHEST, preferred_element_type=F32)


def kernel(
    grad_hbm, mom_hbm, basis_hbm, rows_hbm, wide_hbm, out, grad, mom, basis_t, rows_t, wide_t, give, part,
    far_p, far_m, near_p, near_m, from_z, all_z, left_t, bands, bands_c, bands_z, sums_z, bands_xy, sums_y, bands_h, rest,
    load_sem, core_ss, core_rs, x_ss, x_rs, z_ss, z_rs, b_ss, b_rs, know,
):
    rep, f = lax.axis_index("rep"), lax.axis_index("fsdp")
    zh, y = lax.div(rep, NY), lax.rem(rep, NY)
    zl, x, c = lax.div(f, 2 * NX), lax.rem(lax.div(f, 2), NX), lax.rem(f, 2)

    x_on = [2 * lax.rem(x + i, NX) for i in range(NX)]
    l_on = [2 * NX * lax.rem(zl + i, NL) for i in range(NL)]
    y_on = [lax.rem(y + i, NY) for i in range(NY)]
    h_on = [NY * lax.rem(zh + i, NH) for i in range(NH)]
    c_on = [c, 1 - c]

    def device(dx=0, dy=0, dl=0, dh=0, dc=0):
        return h_on[dh % NH] + y_on[dy % NY], l_on[dl % NL] + x_on[dx % NX] + c_on[dc]

    def signal(sem, **where):
        pl.semaphore_signal(sem, inc=1, device_id=device(**where), device_id_type=MESH)

    def prepare(src, dst, ss, rs, **where):
        return pltpu.make_async_remote_copy(
            src_ref=src, dst_ref=dst, send_sem=ss, recv_sem=rs, device_id=device(**where), device_id_type=MESH
        )

    def send(src, dst, ss, rs, **where):
        copy = prepare(src, dst, ss, rs, **where)
        copy.start()
        return copy

    barrier = pltpu.get_barrier_semaphore()
    inner = (zl == 1) | (zl == 2)
    late = zh >= 2
    edge = ((zh == 2) & (zl == 3)) | ((zh == 3) & (zl == 0))

    @pl.when(late)
    def _():
        for step in (3, 2, 1):
            signal(barrier, dl=step)
        for step in (2, 1, 3):
            signal(barrier, dx=step)
        for step in (2, 1, 3):
            signal(barrier, dy=step)

    @pl.when(jnp.logical_not(late))
    def _():
        for step in (1, 3):
            signal(barrier, dx=step)
            signal(barrier, dy=step)

        @pl.when(zl < 3)
        def _():
            signal(barrier, dl=1)

        @pl.when(zl > 0)
        def _():
            signal(barrier, dl=3)

    signal(barrier, dc=1)

    @pl.when(zh == 0)
    def _():
        for step in (1, 2, 3):
            signal(barrier, dh=step)

    @pl.when(zh == 1)
    def _():
        for step in (1, 2):
            signal(barrier, dh=step)

    def meet(sem):
        @pl.when((zh == 2) & (zl == 3))
        def _():
            signal(sem, dh=1, dl=1)

        @pl.when((zh == 3) & (zl == 0))
        def _():
            signal(sem, dh=3, dl=3)

    meet(barrier)

    def pass_barrier(early):
        if early:
            pl.semaphore_wait(barrier, 6 + lax.rem(lax.div(zl + 1, 2), 2) + zh)
            signal(know.at[3], dx=1)
            signal(know.at[4], dy=1)

            @pl.when(inner)
            def _():
                signal(know.at[5], dl=1)
                signal(know.at[5], dl=3)

        else:
            pl.semaphore_wait(barrier, 12 + jnp.where(edge, 1, 0))
            meet(know.at[3])
            tell_y()
        for step in (1, 2, 3):

            @pl.when((zh >= step) & ((zh < 3) | (step > 1)))
            def _(step=step):
                signal(know.at[0], dh=-step)

    def tell_y():
        for step in (1, 2, 3):
            signal(know.at[2], dx=step)

    def learn_xy():
        pl.semaphore_wait(know.at[3], 1)
        pl.semaphore_wait(know.at[4], 1)
        tell_y()

    def learn_z():
        pl.semaphore_wait(know.at[5], 1)

        @pl.when(zl == 1)
        def _():
            signal(know.at[6], dl=3)

        @pl.when(zl == 2)
        def _():
            signal(know.at[6], dl=1)

        @pl.when(jnp.logical_not(inner))
        def _():
            pl.semaphore_wait(know.at[6], 1)

    def pass_meeting():
        @pl.when(edge)
        def _():
            pl.semaphore_wait(know.at[3], 1)
            for step in (1, 2, 3):
                signal(know.at[4], dl=step)

    def learn_meeting():
        @pl.when(jnp.logical_not(edge))
        def _():
            pl.semaphore_wait(know.at[4], 1)

    loads = [
        pltpu.make_async_copy(grad_hbm.at[0, 0, pl.ds(r0, n)], grad.at[pl.ds(r0, n)], load_sem.at[k])
        for k, (r0, n) in enumerate(PIECES)
    ]
    extra = [
        pltpu.make_async_copy(src, dst, load_sem.at[K + i])
        for i, (src, dst) in enumerate(
            ((basis_hbm, basis_t), (rows_hbm, rows_t), (wide_hbm, wide_t), (mom_hbm.at[0], mom))
        )
    ]
    for copy in [loads[1]] + extra[:3] + [loads[2], loads[0]] + loads[3:] + extra[3:]:
        copy.start()

    def columns(slot, dl, core):
        owner = l_on[dl] + x_on[STEP_OF_SLOT[slot]] + c_on[core]
        return pl.ds(pl.multiple_of(owner * WIDTH, WIDTH), WIDTH)

    def convert(k):
        r0, n = PIECES[k]
        for slot in range(4):
            for dl in range(NL):
                give[slot, dl, pl.ds(r0, n)] = grad[pl.ds(r0, n), columns(slot, dl, 1)].astype(F32)

    def add_own(k, slot):
        r0, n = PIECES[k]
        for dl in range(NL):
            part[slot, dl, pl.ds(r0, n)] += grad[pl.ds(r0, n), columns(slot, dl, 0)].astype(F32)

    sent = []

    def drain():
        while sent:
            sent.pop(0).wait_send()

    core_far, core_rest = {}, {}

    def give_piece(k):
        r0, n = PIECES[k]
        rows = pl.ds(r0, n)
        core_far[k] = send(
            give.at[pl.ds(FAR, 1), :, rows], part.at[pl.ds(FAR, 1), :, rows], core_ss.at[2 * k], core_rs.at[2 * k], dc=1
        )
        core_rest[k] = send(
            give.at[pl.ds(1, 3), :, rows], part.at[pl.ds(1, 3), :, rows], core_ss.at[2 * k + 1], core_rs.at[2 * k + 1], dc=1
        )
        sent.extend((core_far[k], core_rest[k]))

    fars, nears, adds, zs = {}, {}, {}, {}

    def halves(k):
        r0, n = PIECES[k]
        return pl.ds(r0, n // 2), pl.ds(r0 + n // 2, n // 2), pl.ds(r0 // 2, n // 2)

    def members(k):
        return pl.ds(0, 1 if k in Z_FIRST else NL)

    def send_far(k):
        lower, upper, packed = halves(k)
        dls = members(k)
        fars[k] = (
            send(part.at[FAR, dls, lower], far_p.at[dls, packed], x_ss.at[6 * k], x_rs.at[6 * k], dx=1),
            send(part.at[FAR, dls, upper], far_m.at[dls, packed], x_ss.at[6 * k + 1], x_rs.at[6 * k + 1], dx=-1),
        )
        sent.extend(fars[k])

    def send_near(k):
        lower, upper, packed = halves(k)
        dls = members(k)
        nears[k] = (
            send(part.at[NEXT, dls, upper], near_p.at[dls, upper], x_ss.at[6 * k + 2], x_rs.at[6 * k + 2], dx=1),
            send(part.at[PREV, dls, lower], near_m.at[dls, lower], x_ss.at[6 * k + 3], x_rs.at[6 * k + 3], dx=-1),
        )
        sent.extend(nears[k])

    def open_piece(k):
        core_far[k].wait_recv()
        add_own(k, FAR)
        send_far(k)
        core_rest[k].wait_recv()
        add_own(k, NEXT)
        add_own(k, PREV)
        send_near(k)
        add_own(k, OWN)

    def pass_on(k):
        lower, upper, packed = halves(k)
        dls = members(k)
        fars[k][0].wait_recv()
        part[NEXT, dls, lower] += far_p[dls, packed]
        first = send(part.at[NEXT, dls, lower], near_p.at[dls, lower], x_ss.at[6 * k + 4], x_rs.at[6 * k + 4], dx=1)
        fars[k][1].wait_recv()
        part[PREV, dls, upper] += far_m[dls, packed]
        second = send(part.at[PREV, dls, upper], near_m.at[dls, upper], x_ss.at[6 * k + 5], x_rs.at[6 * k + 5], dx=-1)
        adds[k] = (first, second)
        sent.extend(adds[k])

    def along_z(k):
        r0, n = PIECES[k]
        rows = pl.ds(r0, n)
        for copy in nears[k] + adds[k]:
            copy.wait_recv()
        zs[k] = []
        for dl in (3, 2, 1, 0):
            part[OWN, dl, rows] += near_p[dl, rows] + near_m[dl, rows]
            if dl:
                zs[k].append(
                    send(part.at[OWN, dl, rows], from_z.at[dl - 1, rows], z_ss.at[3 * k + dl - 1], z_rs.at[3 * k + dl - 1], dl=dl)
                )
        sent.extend(zs[k])

    def close(k):
        r0, n = PIECES[k]
        rows = pl.ds(r0, n)
        for copy in zs[k]:
            copy.wait_recv()
        out[0, rows] = rest[rows] + ((part[OWN, 0, rows] + from_z[0, rows]) + (from_z[1, rows] + from_z[2, rows]))

    def z_first(k):
        r0, n = PIECES[k]
        rows = pl.ds(r0, n)
        core_far[k].wait_recv()
        core_rest[k].wait_recv()
        for slot in range(4):
            add_own(k, slot)
        zs[k] = [
            send(part.at[:, dl, rows], all_z.at[dl - 1, :, rows], z_ss.at[3 * k + dl - 1], z_rs.at[3 * k + dl - 1], dl=dl)
            for dl in (3, 2, 1)
        ]
        sent.extend(zs[k])

    def x_second(k):
        r0, n = PIECES[k]
        rows = pl.ds(r0, n)
        for copy in zs[k]:
            copy.wait_recv()
        for slot in range(4):
            part[slot, 0, rows] += (all_z[0, slot, rows] + all_z[1, slot, rows]) + all_z[2, slot, rows]
            if slot == FAR:
                send_far(k)
        send_near(k)

    def close_x(k):
        r0, n = PIECES[k]
        rows = pl.ds(r0, n)
        for copy in nears[k] + adds[k]:
            copy.wait_recv()
        out[0, rows] = rest[rows] + (part[OWN, 0, rows] + (near_p[0, rows] + near_m[0, rows]))

    def fold(left):
        high, low = split(jnp.concatenate([left[:8], left[8:]], axis=1))
        return jnp.concatenate([high, low], axis=0)

    def tile(both):
        return (both[:8, :128] + both[:8, 128:]) + both[8:, :128]

    def band_parts():
        step = 4
        for first in range(0, NL * NX * 2, step):
            left = dot(rows_t[...], grad[:, first * WIDTH : (first + step) * WIDTH])
            left = left[:16] + left[16:]
            for i in range(step):
                at = (first + i) * 16
                left_t[at : at + 16] = fold(left[:, i * WIDTH : (i + 1) * WIDTH])
        both = dot(left_t[...], wide_t[...])
        for owner in range(NL * NX * 2):
            which = c_on[owner % 2]
            dl = lax.rem(owner // (2 * NX) - zl + NL, NL)
            bands[which, dl, owner // 2 % NX] = tile(both[owner * 16 : owner * 16 + 16])

    def band_of_momentum():
        high, low = split(mom[...])
        left = dot(rows_t[...], high)
        left = (left[:16] + left[16:]) + dot(rows_t[:16], low)
        return tile(dot(fold(left), wide_t[...]))

    def inverse(coeffs):
        high, low = split(coeffs)
        both = jnp.concatenate([high, low], axis=0)
        dims = (((1,), (1,)), ((), ()))
        one = lax.dot_general(both, wide_t[:, :128], dims, preferred_element_type=F32)
        two = lax.dot_general(both, wide_t[:, 128:], dims, preferred_element_type=F32)
        wide = (one[:8] + one[8:]) + two[:8]
        return [exact(basis_t[...], wide[:, i * WIDTH : (i + 1) * WIDTH], ((0,), (0,))) for i in range(2)]

    def band_core():
        copy = send(bands.at[1], bands_c, b_ss.at[0], b_rs.at[0], dc=1)
        sent.append(copy)
        return [copy]

    def band_z(copies):
        for copy in copies:
            copy.wait_recv()
        bands_c[...] += bands[0]
        copies = [send(bands_c.at[dl], bands_z.at[dl - 1], b_ss.at[dl], b_rs.at[dl], dl=dl) for dl in (2, 3, 1)]
        sent.extend(copies)
        return copies

    def band_xy(copies):
        for copy in copies:
            copy.wait_recv()
        sums_z[...] = (bands_c[0] + bands_z[0]) + (bands_z[1] + bands_z[2])
        sums_z[x] += 0.999 * band_of_momentum()
        bands_xy[y, 0] = sums_z[x]
        pl.semaphore_wait(know.at[2], 3)
        copies = []
        for dx in (2, 1, 3, 0):
            for dy in (2, 1, 3, 0):
                if dx or dy:
                    i = 4 + dx * 4 + dy
                    copies.append(send(sums_z.at[lax.div(x_on[dx], 2)], bands_xy.at[y, dx], b_ss.at[i], b_rs.at[i], dx=dx, dy=dy))
        sent.extend(copies)
        return copies

    def band_y(copies):
        for copy in copies:
            copy.wait_recv()
        for i in range(NY):
            sums_y[i] = (bands_xy[i, 0] + bands_xy[i, 1]) + (bands_xy[i, 2] + bands_xy[i, 3])
        bands_h[zh] = (sums_y[0] + sums_y[1]) + (sums_y[2] + sums_y[3])

    to_h = [None] + [prepare(bands_h.at[zh], bands_h.at[zh], b_ss.at[20 + dh], b_rs.at[20 + dh], dh=dh) for dh in (1, 2, 3)]

    def band_h(first):
        if first == 1:
            to_h[3].start()
        if first < 2:
            pl.semaphore_wait(know.at[0], 3 - first)
        else:
            learn_meeting()
        for dh in (2, 1) if first == 1 else (2, 1, 3):
            to_h[dh].start()

    def find_rest():
        for i, value in enumerate(inverse(sums_y[y])):
            rows = pl.ds(i * GROUP, GROUP)
            rest[rows] = 0.999 * mom[rows] - value

    def band_end():
        for copy in to_h[1:]:
            copy.wait_recv()
        shared = ((bands_h[0] + bands_h[1]) + (bands_h[2] + bands_h[3])) * (1.0 / (NY * NH))
        for i, value in enumerate(inverse(shared)):
            out[1, pl.ds(i * GROUP, GROUP)] = value

    @pl.when(zh == 0)
    def _():
        loads[1].wait()
        convert(1)
        pass_barrier(True)
        give_piece(1)
        for copy in extra[:3] + loads[:1] + loads[2:]:
            copy.wait()
        convert(2)
        give_piece(2)
        convert(0)
        give_piece(0)
        open_piece(1)
        learn_xy()
        convert(3)
        give_piece(3)
        convert(4)
        give_piece(4)
        open_piece(2)
        learn_z()
        z_first(0)
        pass_on(1)
        open_piece(3)
        band_parts()
        b = band_core()
        pass_on(2)
        extra[3].wait()
        b = band_z(b)
        open_piece(4)
        along_z(1)
        pass_on(3)
        b = band_xy(b)
        x_second(0)
        along_z(2)
        pass_on(4)
        pass_on(0)
        along_z(3)
        band_y(b)
        find_rest()
        close(1)
        band_h(0)
        close(2)
        drain()
        along_z(4)
        close_x(0)
        close(3)
        band_end()
        close(4)
        drain()
        for copy in to_h[1:]:
            copy.wait_send()

    @pl.when(zh == 1)
    def _():
        loads[1].wait()
        convert(1)
        pass_barrier(True)
        give_piece(1)
        for copy in extra[:3] + loads[:1] + loads[2:]:
            copy.wait()
        convert(2)
        give_piece(2)
        band_parts()
        b = band_core()
        extra[3].wait()
        open_piece(1)
        learn_xy()
        convert(0)
        give_piece(0)
        convert(3)
        give_piece(3)
        convert(4)
        give_piece(4)
        open_piece(2)
        learn_z()
        b = band_z(b)
        z_first(0)
        b = band_xy(b)
        pass_on(1)
        open_piece(3)
        band_y(b)
        band_h(1)
        pass_on(2)
        find_rest()
        open_piece(4)
        along_z(1)
        pass_on(3)
        x_second(0)
        along_z(2)
        pass_on(4)
        pass_on(0)
        along_z(3)
        close(1)
        close(2)
        drain()
        along_z(4)
        close_x(0)
        close(3)
        band_end()
        close(4)
        drain()
        for copy in to_h[1:]:
            copy.wait_send()

    @pl.when(zh >= 2)
    def _():
        loads[1].wait()
        for copy in extra[:3] + loads[:1] + loads[2:]:
            copy.wait()
        band_parts()
        convert(1)
        pass_barrier(False)
        b = band_core()
        give_piece(1)
        convert(2)
        give_piece(2)
        extra[3].wait()
        b = band_z(b)
        open_piece(1)
        pass_meeting()
        convert(0)
        give_piece(0)
        convert(3)
        give_piece(3)
        convert(4)
        give_piece(4)
        z_first(0)
        b = band_xy(b)
        open_piece(2)
        pass_on(1)
        open_piece(3)
        band_y(b)
        band_h(2)
        pass_on(2)
        find_rest()
        open_piece(4)
        along_z(1)
        pass_on(3)
        x_second(0)
        along_z(2)
        pass_on(4)
        pass_on(0)
        along_z(3)
        close(1)
        close(2)
        drain()
        along_z(4)
        close_x(0)
        close(3)
        band_end()
        close(4)
        drain()
        for copy in to_h[1:]:
            copy.wait_send()


def body(grad_parts, momentum):
    basis, rows, wide = tables()

    def halves(table, axis):
        high = table.astype(jnp.bfloat16)
        low = (table - high.astype(np.float32)).astype(jnp.bfloat16)
        return jnp.asarray(np.concatenate([high, low], axis=axis))

    operands = (grad_parts, momentum, jnp.asarray(basis), halves(rows, 0), halves(wide, 1))
    operands = [pltpu.with_memory_space_constraint(a, pltpu.HBM) for a in operands]
    vmem = pltpu.VMEM
    dma = pltpu.SemaphoreType.DMA
    tile = (8, 128)
    out = pl.pallas_call(
        kernel,
        out_shape=pltpu.VMEM((2, ROWS, WIDTH), F32),
        in_specs=[pl.BlockSpec(memory_space=pltpu.HBM)] * 5,
        out_specs=pl.BlockSpec(memory_space=pltpu.VMEM),
        scratch_shapes=[
            vmem((ROWS, 8192), BF16),
            vmem((ROWS, WIDTH), F32),
            vmem((BAND, GROUP), F32),
            vmem((32, ROWS), BF16),
            vmem((2 * WIDTH, 256), BF16),
            vmem((4, NL, ROWS, WIDTH), F32),
            vmem((4, NL, ROWS, WIDTH), F32),
            vmem((NL, ROWS // 2, WIDTH), F32),
            vmem((NL, ROWS // 2, WIDTH), F32),
            vmem((NL, ROWS, WIDTH), F32),
            vmem((NL, ROWS, WIDTH), F32),
            vmem((3, ROWS, WIDTH), F32),
            vmem((3, 4, Z_ROWS, WIDTH), F32),
            vmem((16 * NL * NX * 2, 2 * WIDTH), BF16),
            vmem((2, NL, NX, *tile), F32),
            vmem((NL, NX, *tile), F32),
            vmem((3, NX, *tile), F32),
            vmem((NX, *tile), F32),
            vmem((NY, NX, *tile), F32),
            vmem((NY, *tile), F32),
            vmem((NH, *tile), F32),
            vmem((ROWS, WIDTH), F32),
            dma((K + 4,)),
            dma((2 * K,)),
            dma((2 * K,)),
            dma((6 * K,)),
            dma((6 * K,)),
            dma((3 * K,)),
            dma((3 * K,)),
            dma((24,)),
            dma((24,)),
            pltpu.SemaphoreType.REGULAR((7,)),
        ],
        compiler_params=pltpu.CompilerParams(collective_id=0, has_side_effects=True, vmem_limit_bytes=56 * 2**20),
    )(*operands)
    return out[0][None], out[1]


def solution(mesh):
    in_specs = (P("rep", "fsdp", None, None), P("rep", None, "fsdp"))
    out_specs = (P("rep", None, "fsdp"), P(None, "fsdp"))
    return jax.shard_map(body, mesh=mesh, in_specs=in_specs, out_specs=out_specs, check_vma=False)
```
